32 devices in a mesh: groups: 2 (over y), gx: 4 (over z), gy: 4 (over x, core).
Axes of the slice: x: 2, y: 2, z: 4, core: 2. Of those that a mesh axis runs over, the one named last changes fastest.
Arguments:
- populations: float32 [19, 64, 64, 128], P(None, ('groups', 'gx'), 'gy'), parts along dimension 1, may hold values from 0 to 1.1, as said below
- fluid_mask: int32 [64, 64, 128], P(('groups', 'gx'), 'gy'), parts along dimension 0, may hold values 0 or 1
- wet_class: int32 [64, 64, 128], P(('groups', 'gx'), 'gy'), parts along dimension 0, may hold values from 0 to 3
- wall_potential: float32 [8], P('groups'), parts along dimension 0, may hold values from 0 to 1
- relax_rates: float32 [19], replicated, may hold values from 0.8 to 1.6
Outputs:
- populations_out: float32 [19, 64, 64, 128], P(None, ('groups', 'gx'), 'gy'), parts along dimension 1
- velocity: float32 [3, 64, 64, 128], P(None, ('groups', 'gx'), 'gy'), parts along dimension 1
The draws below stay inside these ranges and needn't reach their ends.
There are 2 independent parts, one for each index of `groups`. The reference program is written for one: setup_inputs(seed, part) draws one part's arguments, and reference() takes and returns one part's arrays. A program takes and returns all parts, laid end to end along the dimension named above; an argument that names none is the same for every part. Nothing has to cross between parts.
Inputs may be any that keep to these rules, and one draw needn't show every extreme that they name: `populations`: every population is positive.
All inputs are finite; a program needn't handle non-finite values. No bound on the sum of `fluid_mask` on one device may be relied on, other than what follows from the above.
Results may differ from the reference program's by a relative error of at most 0.0003.
Values sent between devices are 32-bit elements; how exact they have to be, the bound alone decides.
A program may use at most 64 MiB of HBM per device.

```python
import math
import jax
import jax.numpy as jnp
import numpy as np
from jax import lax

VELOCITIES = 19
WET_CLASSES = 4
STEPS = 4
SLAB = 128
NX = 32
NY = 64


def draw_populations(key, part):
    key_density, key_jitter = jax.random.split(key, 2)
    weights = jnp.array([1.0 / 3.0] + [1.0 / 18.0] * 6 + [1.0 / 36.0] * 12, jnp.float32)
    jitter = jax.random.uniform(key_jitter, (VELOCITIES, NX, NY, SLAB), jnp.float32, -0.3, 0.3)
    density = jnp.exp(jax.random.uniform(key_density, (NX, NY, SLAB), jnp.float32, jnp.log(0.5), jnp.log(2.0)))
    return weights[:, None, None, None] * density[None] * (1.0 + jitter)


def place_ends(entries, rng, low, high):
    spot = [jax.random.randint(jax.random.fold_in(rng, axis), (), 0, length) for axis, length in enumerate(entries.shape)]
    widest = entries.shape.index(max(entries.shape))
    next_to = spot[:widest] + [(spot[widest] + 1) % entries.shape[widest]] + spot[widest + 1:]
    return entries.at[tuple(spot)].set(low).at[tuple(next_to)].set(high)


def setup_inputs(seed: int = 0, part: int = 0) -> dict:
    key_list = jax.random.split(jax.random.key(seed), 6)
    part_keys = jax.random.split(jax.random.fold_in(key_list[5], part), 6)
    populations = draw_populations(jax.random.fold_in(jax.random.fold_in(key_list[5], part), 71), part)
    fluid_mask = place_ends((jax.random.randint(part_keys[1], (NX, NY, SLAB), 0, 10) < 7).astype(jnp.int32), jax.random.fold_in(part_keys[1], 1), 0, 1)
    wet_class = place_ends(jax.random.randint(part_keys[2], (NX, NY, SLAB), 0, WET_CLASSES), jax.random.fold_in(part_keys[2], 1), 0, WET_CLASSES - 1).astype(jnp.int32)
    wall_potential = jnp.clip(jax.random.uniform(part_keys[3], (WET_CLASSES,), jnp.float32, 0.0, 1.0), 0.0, 1.0)
    relax_rates = jnp.clip(jnp.exp(jax.random.uniform(key_list[4], (VELOCITIES,), jnp.float32, math.log(0.8), math.log(1.6))), 0.8, 1.6)
    return {"populations": populations, "fluid_mask": fluid_mask, "wet_class": wet_class, "wall_potential": wall_potential, "relax_rates": relax_rates}


coupling = -2.5

def lattice():
    velocity_set = np.array([[0, 0, 0], [1, 0, 0], [-1, 0, 0], [0, 1, 0], [0, -1, 0], [0, 0, 1], [0, 0, -1], [1, 1, 0], [-1, -1, 0], [1, -1, 0], [-1, 1, 0], [1, 0, 1], [-1, 0, -1], [1, 0, -1], [-1, 0, 1], [0, 1, 1], [0, -1, -1], [0, 1, -1], [0, -1, 1]])
    weights = [1.0 / 3.0] + [1.0 / 18.0] * 6 + [1.0 / 36.0] * 12
    opposite = [0] + [index + 1 if index % 2 == 1 else index - 1 for index in range(1, 19)]
    lattice_vel = jnp.asarray(velocity_set, jnp.float32)
    along_x = lattice_vel[:, 0]
    along_y = lattice_vel[:, 1]
    along_z = lattice_vel[:, 2]
    moment_basis = jnp.stack([jnp.ones(19, jnp.float32), along_x, along_y, along_z, along_x * along_y, along_x * along_z, along_y * along_z, along_x * along_x, along_y * along_y, along_z * along_z, along_x * along_y * along_y, along_x * along_z * along_z, along_y * along_x * along_x, along_y * along_z * along_z, along_z * along_x * along_x, along_z * along_y * along_y, along_x * along_x * along_y * along_y, along_x * along_x * along_z * along_z, along_y * along_y * along_z * along_z])
    return (velocity_set, weights, opposite, moment_basis)

def collide_matrix(moment_basis, relax_rates):
    gram = jnp.dot(moment_basis, moment_basis.T, precision=lax.Precision.HIGHEST)
    factor = jnp.linalg.cholesky(gram)
    scaled = relax_rates[:, None] * moment_basis
    solved = jax.scipy.linalg.cho_solve((factor, True), scaled)
    return jnp.dot(moment_basis.T, solved, precision=lax.Precision.HIGHEST)

def collision(populations, fluid, potential, near_list, collide, velocity_set, weights):
    pull = [jnp.zeros_like(potential), jnp.zeros_like(potential), jnp.zeros_like(potential)]
    for index in range(1, 19):
        for column in range(3):
            if velocity_set[index][column] != 0:
                pull[column] = pull[column] + float(weights[index] * int(velocity_set[index][column])) * near_list[index]
    force = -coupling * potential[None] * jnp.stack(pull)
    density = jnp.sum(populations, axis=0)
    safe_density = jnp.where(fluid, density, 1.0)
    lattice_vel = jnp.asarray(velocity_set, jnp.float32)
    momentum = jnp.einsum('kc,kxyz->cxyz', lattice_vel, populations, precision=lax.Precision.HIGHEST)
    speed = (momentum + 0.5 * force) / safe_density[None]
    along = jnp.einsum('kc,cxyz->kxyz', lattice_vel, speed, precision=lax.Precision.HIGHEST)
    push = jnp.einsum('kc,cxyz->kxyz', lattice_vel, force, precision=lax.Precision.HIGHEST)
    speed_sq = jnp.sum(speed * speed, axis=0)
    speed_force = jnp.sum(speed * force, axis=0)
    weight_col = jnp.asarray(weights, jnp.float32)[:, None, None, None]
    equil = weight_col * safe_density[None] * (1.0 + 3.0 * along + 4.5 * along * along - 1.5 * speed_sq[None])
    source = weight_col * (3.0 * (push - speed_force[None]) + 9.0 * along * push)
    excess = populations - equil + 0.5 * source
    shape = populations.shape
    relaxed = jnp.dot(collide, excess.reshape(shape[0], -1), precision=lax.Precision.HIGHEST).reshape(shape)
    return (populations + source - relaxed, speed)

def reference(populations, fluid_mask, wet_class, wall_potential, relax_rates):
    velocity_set, weights, opposite, moment_basis = lattice()
    collide = collide_matrix(moment_basis, relax_rates)
    fluid = fluid_mask == 1
    classes = jnp.arange(WET_CLASSES, dtype=jnp.int32)[:, None, None, None]
    wall_values = jnp.sum(jnp.where(wet_class[None] == classes, wall_potential[:, None, None, None], 0.0), axis=0)
    shifts = [tuple((int(value) for value in velocity_set[index])) for index in range(19)]
    inflow = jnp.stack([jnp.roll(fluid, shifts[index], axis=(0, 1, 2)) for index in range(19)])
    speed = None
    for step in range(STEPS):
        density = jnp.sum(populations, axis=0)
        safe_density = jnp.where(fluid, density, 1.0)
        potential = jnp.where(fluid, 1.0 - jnp.exp(-safe_density), wall_values)
        near_list = [None] + [jnp.roll(potential, tuple((-value for value in shifts[index])), axis=(0, 1, 2)) for index in range(1, 19)]
        post, speed = collision(populations, fluid, potential, near_list, collide, velocity_set, weights)
        passed = jnp.stack([jnp.roll(post[index], shifts[index], axis=(0, 1, 2)) for index in range(19)])
        bounced = jnp.stack([post[opposite[index]] for index in range(19)])
        populations = jnp.where(fluid[None], jnp.where(inflow, passed, bounced), 0.0)
    velocity = jnp.where(fluid[None], speed, 0.0)
    return (populations, velocity)
```

```python
import functools

import jax
import jax.numpy as jnp
from jax import lax
from jax.experimental import pallas as pl
from jax.experimental.pallas import tpu as pltpu
from jax.sharding import PartitionSpec as P

WET_CLASSES = 4
STEPS = 4
COUPLING = 2.5
PAD = 8
VEL = [
    (0, 0, 0),
    (1, 0, 0),
    (-1, 0, 0),
    (0, 1, 0),
    (0, -1, 0),
    (0, 0, 1),
    (0, 0, -1),
    (1, 1, 0),
    (-1, -1, 0),
    (1, -1, 0),
    (-1, 1, 0),
    (1, 0, 1),
    (-1, 0, -1),
    (1, 0, -1),
    (-1, 0, 1),
    (0, 1, 1),
    (0, -1, -1),
    (0, 1, -1),
    (0, -1, 1),
]
INDEX = {v: k for k, v in enumerate(VEL)}
OPP = [INDEX[(-a, -b, -c)] for a, b, c in VEL]
ORDER = (
    [k for k in range(19) if VEL[k][0] == 1]
    + [k for k in range(19) if VEL[k][0] == -1]
    + [k for k in range(19) if VEL[k][0] == 0]
)
PLACE = [ORDER.index(k) for k in range(19)]
CROSS = [[k for k in range(19) if VEL[k][1] == s] for s in (-1, 1)]
CORNERS = [(1, 1), (1, -1), (-1, 1), (-1, -1)]
SENDS = [(1, 0), (-1, 0), (0, 1), (0, -1)] + CORNERS


def roll_z(value, step):
    if step == 0:
        return value
    return pltpu.roll(value, step % value.shape[-1], axis=value.ndim - 1)


def to_moments(f):
    g = lambda *v: f[INDEX[v]]
    m = {}

    def plane(pp, mm, pm, mp):
        a, b, c, d = pp + mm, pm + mp, pp - mm, pm - mp
        return a + b, a - b, c + d, c - d

    m["xxyy"], m["xy"], m["xyy"], m["yxx"] = plane(
        g(1, 1, 0), g(-1, -1, 0), g(1, -1, 0), g(-1, 1, 0)
    )
    m["xxzz"], m["xz"], m["xzz"], m["zxx"] = plane(
        g(1, 0, 1), g(-1, 0, -1), g(1, 0, -1), g(-1, 0, 1)
    )
    m["yyzz"], m["yz"], m["yzz"], m["zyy"] = plane(
        g(0, 1, 1), g(0, -1, -1), g(0, 1, -1), g(0, -1, 1)
    )
    sx, dx = f[1] + f[2], f[1] - f[2]
    sy, dy = f[3] + f[4], f[3] - f[4]
    sz, dz = f[5] + f[6], f[5] - f[6]
    m["xx"] = sx + (m["xxyy"] + m["xxzz"])
    m["yy"] = sy + (m["xxyy"] + m["yyzz"])
    m["zz"] = sz + (m["xxzz"] + m["yyzz"])
    m["x"] = dx + (m["xyy"] + m["xzz"])
    m["y"] = dy + (m["yxx"] + m["yzz"])
    m["z"] = dz + (m["zxx"] + m["zyy"])
    m["1"] = ((f[0] + sx) + (sy + sz)) + ((m["xxyy"] + m["xxzz"]) + m["yyzz"])
    return m


def from_moments(m):
    f = [None] * 19

    def plane(even, cross, first, second, v):
        a, b = 0.25 * (even + cross), 0.25 * (even - cross)
        c, d = 0.25 * (first + second), 0.25 * (first - second)
        values = (a + c, a - c, b + d, b - d)
        for velocity, value in zip(v, values):
            f[INDEX[velocity]] = value

    plane(m["xxyy"], m["xy"], m["xyy"], m["yxx"], [(1, 1, 0), (-1, -1, 0), (1, -1, 0), (-1, 1, 0)])
    plane(m["xxzz"], m["xz"], m["xzz"], m["zxx"], [(1, 0, 1), (-1, 0, -1), (1, 0, -1), (-1, 0, 1)])
    plane(m["yyzz"], m["yz"], m["yzz"], m["zyy"], [(0, 1, 1), (0, -1, -1), (0, 1, -1), (0, -1, 1)])
    sx = m["xx"] - (m["xxyy"] + m["xxzz"])
    sy = m["yy"] - (m["xxyy"] + m["yyzz"])
    sz = m["zz"] - (m["xxzz"] + m["yyzz"])
    dx = m["x"] - (m["xyy"] + m["xzz"])
    dy = m["y"] - (m["yxx"] + m["yzz"])
    dz = m["z"] - (m["zxx"] + m["zyy"])
    f[1], f[2] = 0.5 * (sx + dx), 0.5 * (sx - dx)
    f[3], f[4] = 0.5 * (sy + dy), 0.5 * (sy - dy)
    f[5], f[6] = 0.5 * (sz + dz), 0.5 * (sz - dz)
    f[0] = (m["1"] - (sx + sy)) - (sz + ((m["xxyy"] + m["xxzz"]) + m["yyzz"]))
    return f


NAMES = [
    "1", "x", "y", "z", "xy", "xz", "yz", "xx", "yy", "zz",
    "xyy", "xzz", "yxx", "yzz", "zxx", "zyy", "xxyy", "xxzz", "yyzz",
]


def collide(f, fluid, near, rates):
    third = 1.0 / 3.0
    m = to_moments(f)
    here = near(0, 0)
    xp, xm, yp, ym = near(1, 0), near(-1, 0), near(0, 1), near(0, -1)
    dx, dy = xp - xm, yp - ym
    ring = (2.0 * here + (xp + xm)) + (yp + ym)
    pp, pm, mp, mm = near(1, 1), near(1, -1), near(-1, 1), near(-1, -1)
    a, b = pp - mm, pm - mp
    scale = (COUPLING / 36.0) * here
    fx = scale * ((2.0 * dx + (a + b)) + (roll_z(dx, 1) + roll_z(dx, -1)))
    fy = scale * ((2.0 * dy + (a - b)) + (roll_z(dy, 1) + roll_z(dy, -1)))
    fz = scale * (roll_z(ring, -1) - roll_z(ring, 1))
    rho = jnp.where(fluid, m["1"], 1.0)
    inv = 1.0 / rho
    ux, uy, uz = ((m[n] + 0.5 * v) * inv for n, v in (("x", fx), ("y", fy), ("z", fz)))
    jx, jy, jz = rho * ux, rho * uy, rho * uz
    qx, qy, qz = jx * ux, jy * uy, jz * uz
    wx, wy, wz = ux * fx, uy * fy, uz * fz
    rho3, rho9 = rho * third, rho * (1.0 / 9.0)
    hx, hy, hz = (0.5 * q for q in (qx, qy, qz))
    hsum = rho9 - third * (hx + hy + hz)
    wsum = third * (wx + wy + wz)
    equil = {
        "1": rho, "x": jx, "y": jy, "z": jz,
        "xy": jx * uy, "xz": jx * uz, "yz": jy * uz,
        "xx": rho3 + qx, "yy": rho3 + qy, "zz": rho3 + qz,
        "xyy": jx * third, "yxx": jy * third, "zxx": jz * third,
        "xxyy": hsum + (hx + hy), "xxzz": hsum + (hx + hz), "yyzz": hsum + (hy + hz),
    }
    source = {
        "1": None, "x": fx, "y": fy, "z": fz,
        "xy": fx * uy + fy * ux, "xz": fx * uz + fz * ux, "yz": fy * uz + fz * uy,
        "xx": 2.0 * wx, "yy": 2.0 * wy, "zz": 2.0 * wz,
        "xyy": fx * third, "yxx": fy * third, "zxx": fz * third,
        "xxyy": (wx + wy) - wsum, "xxzz": (wx + wz) - wsum, "yyzz": (wy + wz) - wsum,
    }
    for table in (equil, source):
        table["xzz"], table["yzz"], table["zyy"] = table["xyy"], table["yxx"], table["zxx"]
    after = {}
    for row, name in enumerate(NAMES):
        rate = rates[row]
        if source[name] is None:
            after[name] = m[name] + rate * (equil[name] - m[name])
        else:
            after[name] = (m[name] + source[name]) + rate * (
                (equil[name] - m[name]) - 0.5 * source[name]
            )
    return from_moments(after), (ux, uy, uz)


def kernel(
    counts, pop_ref, mask_ref, wet_ref, wall_ref, rate_ref, out_ref, vel_ref,
    pot, f_buf, bits, post, pot_ysend, pot_yrecv, pot_crecv, ysend, yrecv, crecv,
    send_sem, recv_sem,
):
    nx, ny = mask_ref.shape[0], mask_ref.shape[1]
    halves = ny // 8
    top = PAD + ny
    gx, gy = lax.axis_index("gx"), lax.axis_index("gy")

    def neighbour(d):
        return {
            "gx": lax.rem(gx + d[0] + counts[0], counts[0]),
            "gy": lax.rem(gy + d[1] + counts[1], counts[1]),
        }

    barrier = pltpu.get_barrier_semaphore()
    for d in SENDS:
        pl.semaphore_signal(
            barrier, inc=1, device_id=neighbour(d), device_id_type=pl.DeviceIdType.MESH
        )

    def copies(kind, slot, pairs):
        made = []
        for i, d in enumerate(SENDS):
            made.append(
                pltpu.make_async_remote_copy(
                    src_ref=pairs[d][0],
                    dst_ref=pairs[d][1],
                    send_sem=send_sem.at[kind, slot, i],
                    recv_sem=recv_sem.at[kind, slot, i],
                    device_id=neighbour(d),
                    device_id_type=pl.DeviceIdType.MESH,
                )
            )
        return made

    rows = pl.ds(PAD, ny)

    def pot_copies(slot, wide):
        parts = pl.ds(0, 2 if wide else 1)
        pairs = {
            (1, 0): (pot.at[slot, parts, nx, rows], pot.at[slot, parts, 0, rows]),
            (-1, 0): (pot.at[slot, parts, 1, rows], pot.at[slot, parts, nx + 1, rows]),
        }
        for side, s in enumerate((-1, 1)):
            tile = pot_ysend.at[slot, side, parts]
            pairs[(0, s)] = (tile, pot_yrecv.at[slot, side, parts])
            for c, d in enumerate(CORNERS):
                if d[1] == s:
                    pairs[d] = (tile, pot_crecv.at[slot, c, parts])
        return copies(0, slot, pairs)

    def post_copies(slot):
        ahead, back = pl.ds(0, 5), pl.ds(5, 5)
        pairs = {
            (1, 0): (post.at[slot, ahead, nx, rows], post.at[slot, ahead, 0, rows]),
            (-1, 0): (post.at[slot, back, 1, rows], post.at[slot, back, nx + 1, rows]),
        }
        for side, s in enumerate((-1, 1)):
            pairs[(0, s)] = (ysend.at[slot, side], yrecv.at[slot, side])
            for c, d in enumerate(CORNERS):
                if d[1] == s:
                    j = CROSS[side].index(INDEX[(d[0], d[1], 0)])
                    pairs[d] = (ysend.at[slot, side, j], crecv.at[slot, c])
        return copies(1, slot, pairs)

    def pot_unpack(slot, wide):
        for part in range(2 if wide else 1):
            for side, ghost in enumerate((top, PAD - 1)):
                for x in range(nx):
                    pot[slot, part, x + 1, ghost : ghost + 1, :] = pot_yrecv[
                        slot, side, part, x : x + 1, :
                    ]
            for c, (dx, dy) in enumerate(CORNERS):
                row = nx - 1 if dx == 1 else 0
                ghost = PAD - 1 if dy == 1 else top
                pot[slot, part, 0 if dx == 1 else nx + 1, ghost : ghost + 1, :] = pot_crecv[
                    slot, c, part, row : row + 1, :
                ]

    def post_unpack(slot):
        for side, ghost in enumerate((top, PAD - 1)):
            for j, k in enumerate(CROSS[side]):
                for x in range(nx):
                    post[slot, PLACE[k], x + 1, ghost : ghost + 1, :] = yrecv[
                        slot, side, j, x : x + 1, :
                    ]
        for c, (dx, dy) in enumerate(CORNERS):
            row = nx - 1 if dx == 1 else 0
            ghost = PAD - 1 if dy == 1 else top
            k = INDEX[(dx, dy, 0)]
            post[slot, PLACE[k], 0 if dx == 1 else nx + 1, ghost : ghost + 1, :] = crecv[
                slot, c, row : row + 1, :
            ]

    def each_block(body):
        def plane(x, carry):
            for h in range(halves):
                body(x, h)
            return carry

        lax.fori_loop(0, nx, plane, 0)

    def put_edges(target, x, h, value):
        if h == 0:
            target(0)[pl.ds(x, 1), :] = value[0:1]
        if h == halves - 1:
            target(1)[pl.ds(x, 1), :] = value[7:8]

    def potential(slot, x, h, f, wide):
        block = pl.ds(8 * h, 8)
        fluid = mask_ref[x, block, :] == 1
        density = f[0]
        for k in range(1, 19):
            density = density + f[k]
        wet = wet_ref[x, block, :]
        wall = jnp.zeros_like(density)
        for c in range(WET_CLASSES):
            wall = wall + jnp.where(wet == c, wall_ref[c], 0.0)
        safe = jnp.where(fluid, density, 1.0)
        value = jnp.where(fluid, 1.0 - jnp.exp(-safe), wall)
        pot[slot, 0, x + 1, pl.ds(PAD + 8 * h, 8), :] = value
        put_edges(lambda side: pot_ysend.at[slot, side, 0], x, h, value)
        if wide:
            flag = jnp.where(fluid, 1.0, 0.0)
            pot[slot, 1, x + 1, pl.ds(PAD + 8 * h, 8), :] = flag
            put_edges(lambda side: pot_ysend.at[slot, side, 1], x, h, flag)

    def streamed(slot, x, h):
        flags = bits[x, pl.ds(8 * h, 8), :]
        f = []
        for k, (ex, ey, ez) in enumerate(VEL):
            if k == 0:
                f.append(post[slot, PLACE[0], x + 1, pl.ds(PAD + 8 * h, 8), :])
                continue
            passed = roll_z(post[slot, PLACE[k], x + 1 - ex, pl.ds(PAD + 8 * h - ey, 8), :], ez)
            bounced = post[slot, PLACE[OPP[k]], x + 1, pl.ds(PAD + 8 * h, 8), :]
            f.append(jnp.where((flags & (1 << k)) != 0, passed, bounced))
        return f

    def first(x, h):
        potential(0, x, h, [pop_ref[k, x, pl.ds(8 * h, 8), :] for k in range(19)], True)

    def inflow(x, h):
        flags = jnp.zeros((8, mask_ref.shape[2]), jnp.int32)
        for k, (ex, ey, ez) in enumerate(VEL):
            if k > 0:
                flag = roll_z(pot[0, 1, x + 1 - ex, pl.ds(PAD + 8 * h - ey, 8), :], ez)
                flags = flags | jnp.where(flag == 1.0, 1 << k, 0)
        bits[x, pl.ds(8 * h, 8), :] = flags

    def collision(step, x, h):
        slot = step % 2
        block = pl.ds(8 * h, 8)
        source = pop_ref if step == 0 else f_buf
        fluid = mask_ref[x, block, :] == 1
        near = lambda dx, dy: pot[slot, 0, x + 1 + dx, pl.ds(PAD + 8 * h + dy, 8), :]
        rates = [rate_ref[r] for r in range(19)]
        f, speed = collide([source[k, x, block, :] for k in range(19)], fluid, near, rates)
        for k in range(19):
            post[slot, PLACE[k], x + 1, pl.ds(PAD + 8 * h, 8), :] = f[k]
            for side in range(2):
                if k in CROSS[side] and h == (0, halves - 1)[side]:
                    row = (0, 7)[side]
                    ysend[slot, side, CROSS[side].index(k), pl.ds(x, 1), :] = f[k][row : row + 1]
        if step == STEPS - 1:
            for c in range(3):
                vel_ref[c, x, block, :] = jnp.where(fluid, speed[c], 0.0)

    def stream(step, x, h):
        f = streamed((step - 1) % 2, x, h)
        for k in range(19):
            f_buf[k, x, pl.ds(8 * h, 8), :] = f[k]
        potential(step % 2, x, h, f, False)

    def last(x, h):
        f = streamed((STEPS - 1) % 2, x, h)
        block = pl.ds(8 * h, 8)
        fluid = mask_ref[x, block, :] == 1
        for k in range(19):
            out_ref[k, x, block, :] = jnp.where(fluid, f[k], 0.0)

    each_block(first)
    pl.semaphore_wait(barrier, len(SENDS))
    for step in range(STEPS):
        slot = step % 2
        if step > 0:
            each_block(functools.partial(stream, step))
        moving = pot_copies(slot, step == 0)
        for copy in moving:
            copy.start()
        for copy in moving:
            copy.wait()
        pot_unpack(slot, step == 0)
        if step == 0:
            each_block(inflow)
        each_block(functools.partial(collision, step))
        moving = post_copies(slot)
        for copy in moving:
            copy.start()
        for copy in moving:
            copy.wait()
        post_unpack(slot)
    each_block(last)


def per_device(counts, populations, fluid_mask, wet_class, wall_potential, relax_rates):
    nx, ny, nz = fluid_mask.shape
    vmem = pl.BlockSpec(memory_space=pltpu.VMEM)
    smem = pl.BlockSpec(memory_space=pltpu.SMEM)
    f32 = jnp.float32
    padded = (nx + 2, ny + 2 * PAD, nz)
    return pl.pallas_call(
        functools.partial(kernel, counts),
        out_shape=(
            jax.ShapeDtypeStruct((19, nx, ny, nz), f32),
            jax.ShapeDtypeStruct((3, nx, ny, nz), f32),
        ),
        in_specs=[vmem, vmem, vmem, smem, smem],
        out_specs=(vmem, vmem),
        scratch_shapes=[
            pltpu.VMEM((2, 2) + padded, f32),
            pltpu.VMEM((19, nx, ny, nz), f32),
            pltpu.VMEM((nx, ny, nz), jnp.int32),
            pltpu.VMEM((2, 19) + padded, f32),
            pltpu.VMEM((2, 2, 2, nx, nz), f32),
            pltpu.VMEM((2, 2, 2, nx, nz), f32),
            pltpu.VMEM((2, 4, 2, nx, nz), f32),
            pltpu.VMEM((2, 2, 5, nx, nz), f32),
            pltpu.VMEM((2, 2, 5, nx, nz), f32),
            pltpu.VMEM((2, 4, nx, nz), f32),
            pltpu.SemaphoreType.DMA((2, 2, len(SENDS))),
            pltpu.SemaphoreType.DMA((2, 2, len(SENDS))),
        ],
        compiler_params=pltpu.CompilerParams(
            collective_id=0, has_side_effects=True, vmem_limit_bytes=48 * 1024 * 1024
        ),
    )(populations, fluid_mask, wet_class, wall_potential, relax_rates)


def solution(mesh):
    counts = (mesh.shape["gx"], mesh.shape["gy"])
    return jax.shard_map(
        functools.partial(per_device, counts),
        mesh=mesh,
        in_specs=(
            P(None, ("groups", "gx"), "gy", None),
            P(("groups", "gx"), "gy", None),
            P(("groups", "gx"), "gy", None),
            P("groups"),
            P(),
        ),
        out_specs=(P(None, ("groups", "gx"), "gy", None), P(None, ("groups", "gx"), "gy", None)),
        check_vma=False,
    )
```

```python
import functools

import jax
import jax.numpy as jnp
from jax import lax
from jax.experimental import pallas as pl
from jax.experimental.pallas import tpu as pltpu
from jax.sharding import PartitionSpec as P

WET_CLASSES = 4
STEPS = 4
COUPLING = 2.5
PAD = 8
VEL = [
    (0, 0, 0),
    (1, 0, 0),
    (-1, 0, 0),
    (0, 1, 0),
    (0, -1, 0),
    (0, 0, 1),
    (0, 0, -1),
    (1, 1, 0),
    (-1, -1, 0),
    (1, -1, 0),
    (-1, 1, 0),
    (1, 0, 1),
    (-1, 0, -1),
    (1, 0, -1),
    (-1, 0, 1),
    (0, 1, 1),
    (0, -1, -1),
    (0, 1, -1),
    (0, -1, 1),
]
INDEX = {v: k for k, v in enumerate(VEL)}
OPP = [INDEX[(-a, -b, -c)] for a, b, c in VEL]
ORDER = (
    [k for k in range(19) if VEL[k][0] == 1]
    + [k for k in range(19) if VEL[k][0] == -1]
    + [k for k in range(19) if VEL[k][0] == 0]
)
PLACE = [ORDER.index(k) for k in range(19)]
CROSS = [[k for k in range(19) if VEL[k][1] == s] for s in (-1, 1)]
CORNERS = [(1, 1), (1, -1), (-1, 1), (-1, -1)]
SENDS = [(1, 0), (-1, 0), (0, 1), (0, -1)] + CORNERS


def roll_z(value, step):
    if step == 0:
        return value
    return pltpu.roll(value, step % value.shape[-1], axis=value.ndim - 1)


def to_moments(f):
    g = lambda *v: f[INDEX[v]]
    m = {}

    def plane(pp, mm, pm, mp):
        a, b, c, d = pp + mm, pm + mp, pp - mm, pm - mp
        return a + b, a - b, c + d, c - d

    m["xxyy"], m["xy"], m["xyy"], m["yxx"] = plane(
        g(1, 1, 0), g(-1, -1, 0), g(1, -1, 0), g(-1, 1, 0)
    )
    m["xxzz"], m["xz"], m["xzz"], m["zxx"] = plane(
        g(1, 0, 1), g(-1, 0, -1), g(1, 0, -1), g(-1, 0, 1)
    )
    m["yyzz"], m["yz"], m["yzz"], m["zyy"] = plane(
        g(0, 1, 1), g(0, -1, -1), g(0, 1, -1), g(0, -1, 1)
    )
    sx, dx = f[1] + f[2], f[1] - f[2]
    sy, dy = f[3] + f[4], f[3] - f[4]
    sz, dz = f[5] + f[6], f[5] - f[6]
    m["xx"] = sx + (m["xxyy"] + m["xxzz"])
    m["yy"] = sy + (m["xxyy"] + m["yyzz"])
    m["zz"] = sz + (m["xxzz"] + m["yyzz"])
    m["x"] = dx + (m["xyy"] + m["xzz"])
    m["y"] = dy + (m["yxx"] + m["yzz"])
    m["z"] = dz + (m["zxx"] + m["zyy"])
    m["1"] = ((f[0] + sx) + (sy + sz)) + ((m["xxyy"] + m["xxzz"]) + m["yyzz"])
    return m


def from_moments(m):
    f = [None] * 19

    def plane(even, cross, first, second, v):
        a, b = 0.25 * (even + cross), 0.25 * (even - cross)
        c, d = 0.25 * (first + second), 0.25 * (first - second)
        values = (a + c, a - c, b + d, b - d)
        for velocity, value in zip(v, values):
            f[INDEX[velocity]] = value

    plane(m["xxyy"], m["xy"], m["xyy"], m["yxx"], [(1, 1, 0), (-1, -1, 0), (1, -1, 0), (-1, 1, 0)])
    plane(m["xxzz"], m["xz"], m["xzz"], m["zxx"], [(1, 0, 1), (-1, 0, -1), (1, 0, -1), (-1, 0, 1)])
    plane(m["yyzz"], m["yz"], m["yzz"], m["zyy"], [(0, 1, 1), (0, -1, -1), (0, 1, -1), (0, -1, 1)])
    sx = m["xx"] - (m["xxyy"] + m["xxzz"])
    sy = m["yy"] - (m["xxyy"] + m["yyzz"])
    sz = m["zz"] - (m["xxzz"] + m["yyzz"])
    dx = m["x"] - (m["xyy"] + m["xzz"])
    dy = m["y"] - (m["yxx"] + m["yzz"])
    dz = m["z"] - (m["zxx"] + m["zyy"])
    f[1], f[2] = 0.5 * (sx + dx), 0.5 * (sx - dx)
    f[3], f[4] = 0.5 * (sy + dy), 0.5 * (sy - dy)
    f[5], f[6] = 0.5 * (sz + dz), 0.5 * (sz - dz)
    f[0] = (m["1"] - (sx + sy)) - (sz + ((m["xxyy"] + m["xxzz"]) + m["yyzz"]))
    return f


NAMES = [
    "1", "x", "y", "z", "xy", "xz", "yz", "xx", "yy", "zz",
    "xyy", "xzz", "yxx", "yzz", "zxx", "zyy", "xxyy", "xxzz", "yyzz",
]


def collide(f, fluid, near, rates):
    third = 1.0 / 3.0
    m = to_moments(f)
    here = near(0, 0)
    xp, xm, yp, ym = near(1, 0), near(-1, 0), near(0, 1), near(0, -1)
    dx, dy = xp - xm, yp - ym
    ring = (2.0 * here + (xp + xm)) + (yp + ym)
    pp, pm, mp, mm = near(1, 1), near(1, -1), near(-1, 1), near(-1, -1)
    a, b = pp - mm, pm - mp
    scale = (COUPLING / 36.0) * here
    fx = scale * ((2.0 * dx + (a + b)) + (roll_z(dx, 1) + roll_z(dx, -1)))
    fy = scale * ((2.0 * dy + (a - b)) + (roll_z(dy, 1) + roll_z(dy, -1)))
    fz = scale * (roll_z(ring, -1) - roll_z(ring, 1))
    rho = jnp.where(fluid, m["1"], 1.0)
    inv = 1.0 / rho
    ux, uy, uz = ((m[n] + 0.5 * v) * inv for n, v in (("x", fx), ("y", fy), ("z", fz)))
    jx, jy, jz = rho * ux, rho * uy, rho * uz
    qx, qy, qz = jx * ux, jy * uy, jz * uz
    wx, wy, wz = ux * fx, uy * fy, uz * fz
    rho3, rho9 = rho * third, rho * (1.0 / 9.0)
    hx, hy, hz = (0.5 * q for q in (qx, qy, qz))
    hsum = rho9 - third * (hx + hy + hz)
    wsum = third * (wx + wy + wz)
    equil = {
        "1": rho, "x": jx, "y": jy, "z": jz,
        "xy": jx * uy, "xz": jx * uz, "yz": jy * uz,
        "xx": rho3 + qx, "yy": rho3 + qy, "zz": rho3 + qz,
        "xyy": jx * third, "yxx": jy * third, "zxx": jz * third,
        "xxyy": hsum + (hx + hy), "xxzz": hsum + (hx + hz), "yyzz": hsum + (hy + hz),
    }
    source = {
        "1": None, "x": fx, "y": fy, "z": fz,
        "xy": fx * uy + fy * ux, "xz": fx * uz + fz * ux, "yz": fy * uz + fz * uy,
        "xx": 2.0 * wx, "yy": 2.0 * wy, "zz": 2.0 * wz,
        "xyy": fx * third, "yxx": fy * third, "zxx": fz * third,
        "xxyy": (wx + wy) - wsum, "xxzz": (wx + wz) - wsum, "yyzz": (wy + wz) - wsum,
    }
    for table in (equil, source):
        table["xzz"], table["yzz"], table["zyy"] = table["xyy"], table["yxx"], table["zxx"]
    after = {}
    for row, name in enumerate(NAMES):
        rate = rates[row]
        if source[name] is None:
            after[name] = m[name] + rate * (equil[name] - m[name])
        else:
            after[name] = (m[name] + source[name]) + rate * (
                (equil[name] - m[name]) - 0.5 * source[name]
            )
    return from_moments(after), (ux, uy, uz)


def kernel(
    counts, pop_hbm, mask_hbm, wet_hbm, wall_hbm, rate_hbm, out_ref, vel_ref,
    pop_ref, mask_ref, wet_ref, wall_ref, rate_ref,
    pot, f_buf, dens, bits, post, pot_ysend, pot_yrecv, pot_crecv,
    xa_recv, ya_send, ya_recv, xb_send, xb_recv, yb_send, yb_recv, cb_send, cb_recv,
    ox, oy, gx_d, gy_d, y_tile,
    in_sem, pot_send_sem, pot_recv_sem, send_sem, recv_sem,
):
    nx, ny, nz = mask_ref.shape
    halves = ny // 8
    top = PAD + ny
    gx, gy = lax.axis_index("gx"), lax.axis_index("gy")
    SIGN = (-1, 1)
    leave_x, leave_y = (0, nx - 1), (0, ny - 1)
    enter_x, enter_y = (nx - 1, 0), (ny - 1, 0)
    ghost_x, ghost_y = (nx + 1, 0), (top, PAD - 1)
    XK = [ORDER[5:10], ORDER[0:5]]

    fetches = [
        pltpu.make_async_copy(a, b, in_sem.at[i])
        for i, (a, b) in enumerate(
            [
                (pop_hbm, pop_ref),
                (mask_hbm, mask_ref),
                (wet_hbm, wet_ref),
                (wall_hbm, wall_ref),
                (rate_hbm, rate_ref),
            ]
        )
    ]
    for copy in fetches:
        copy.start()

    def neighbour(d):
        return {
            "gx": lax.rem(gx + d[0] + counts[0], counts[0]),
            "gy": lax.rem(gy + d[1] + counts[1], counts[1]),
        }

    barrier = pltpu.get_barrier_semaphore()
    for d in SENDS:
        pl.semaphore_signal(
            barrier, inc=1, device_id=neighbour(d), device_id_type=pl.DeviceIdType.MESH
        )

    def remote(src, dst, sent, received, d):
        return pltpu.make_async_remote_copy(
            src_ref=src,
            dst_ref=dst,
            send_sem=sent,
            recv_sem=received,
            device_id=neighbour(d),
            device_id_type=pl.DeviceIdType.MESH,
        )

    rows = pl.ds(PAD, ny)
    xrows = pl.ds(PAD, nx)

    def pot_copies():
        pairs = {
            (1, 0): (pot.at[:, nx, rows], pot.at[:, 0, rows]),
            (-1, 0): (pot.at[:, 1, rows], pot.at[:, nx + 1, rows]),
        }
        for side, s in enumerate(SIGN):
            pairs[(0, s)] = (pot_ysend.at[side], pot_yrecv.at[side])
            for c, d in enumerate(CORNERS):
                if d[1] == s:
                    pairs[d] = (pot_ysend.at[side], pot_crecv.at[c])
        return [
            remote(*pairs[d], pot_send_sem.at[i], pot_recv_sem.at[i], d)
            for i, d in enumerate(SENDS)
        ]

    def a_copies(step):
        p = step % 2
        made = []
        for m, s in enumerate(SIGN):
            part = pl.ds(5 * (1 - m), 5)
            made.append(
                remote(
                    post.at[p, part, leave_x[m] + 1, rows], xa_recv.at[step, m, :, rows],
                    send_sem.at[step, m], recv_sem.at[step, m], (s, 0),
                )
            )
            made.append(
                remote(
                    ya_send.at[step, m, :, xrows], ya_recv.at[step, m, :, xrows],
                    send_sem.at[step, 2 + m], recv_sem.at[step, 2 + m], (0, s),
                )
            )
        return made

    def b_copies(step):
        made = []
        if step < STEPS - 1:
            for m, s in enumerate(SIGN):
                made.append(
                    remote(
                        xb_send.at[step, m], xb_recv.at[step, m],
                        send_sem.at[step, 4 + m], recv_sem.at[step, 4 + m], (s, 0),
                    )
                )
                made.append(
                    remote(
                        yb_send.at[step, m], yb_recv.at[step, m],
                        send_sem.at[step, 6 + m], recv_sem.at[step, 6 + m], (0, s),
                    )
                )
        for c, d in enumerate(CORNERS):
            made.append(
                remote(
                    cb_send.at[step, c], cb_recv.at[step, c],
                    send_sem.at[step, 8 + c], recv_sem.at[step, 8 + c], d,
                )
            )
        return made

    def clear():
        tile = jnp.zeros((8, nz), jnp.float32)
        for p in range(2):
            for m in range(2):
                for k in XK[m]:
                    for r in range((ny + 2 * PAD) // 8):
                        post[p, PLACE[k], ghost_x[m], pl.ds(8 * r, 8), :] = tile
                for k in CROSS[m]:
                    for x in range(nx):
                        post[p, PLACE[k], x + 1, pl.ds((top, 0)[m], 8), :] = tile
        for step in range(STEPS):
            for m in range(2):
                for j in range(5):
                    for r in (0, top):
                        xa_recv[step, m, j, pl.ds(r, 8), :] = tile
                    for r in (0, PAD + nx):
                        ya_send[step, m, j, pl.ds(r, 8), :] = tile
                        ya_recv[step, m, j, pl.ds(r, 8), :] = tile
                for r in range(halves):
                    xb_send[step, m, 1, pl.ds(8 * r, 8), :] = tile
                yb_send[step, m, 1] = jnp.zeros((nx, nz), jnp.float32)
            for c in range(4):
                cb_send[step, c] = tile

    def pot_unpack():
        for part in range(2):
            for m in range(2):
                for x in range(nx):
                    pot[part, x + 1, pl.ds(ghost_y[m], 1), :] = pot_yrecv[m, part, pl.ds(x, 1), :]
            for c, (sx, sy) in enumerate(CORNERS):
                mx, my = (sx + 1) // 2, (sy + 1) // 2
                pot[part, ghost_x[mx], pl.ds(ghost_y[my], 1), :] = pot_crecv[
                    c, part, pl.ds(leave_x[mx], 1), :
                ]

    def each_block(body):
        def plane(x, carry):
            for h in range(halves):
                body(x, h)
            return carry

        lax.fori_loop(0, nx, plane, 0)

    def first(x, h):
        block = pl.ds(8 * h, 8)
        fluid = mask_ref[x, block, :] == 1
        density = pop_ref[0, x, block, :]
        for k in range(1, 19):
            density = density + pop_ref[k, x, block, :]
        wet = wet_ref[x, block, :]
        wall = jnp.zeros_like(density)
        for c in range(WET_CLASSES):
            wall = wall + jnp.where(wet == c, wall_ref[c], 0.0)
        safe = jnp.where(fluid, density, 1.0)
        flag = jnp.where(fluid, 1.0, 0.0)
        for part, value in enumerate((jnp.where(fluid, 1.0 - jnp.exp(-safe), wall), flag)):
            pot[part, x + 1, pl.ds(PAD + 8 * h, 8), :] = value
            for m in range(2):
                if h == leave_y[m] // 8:
                    row = leave_y[m] % 8
                    pot_ysend[m, part, pl.ds(x, 1), :] = value[row : row + 1]

    def inflow(x, h):
        flags = jnp.zeros((8, nz), jnp.int32)
        for k, (ex, ey, ez) in enumerate(VEL):
            if k > 0:
                flag = roll_z(pot[1, x + 1 - ex, pl.ds(PAD + 8 * h - ey, 8), :], ez)
                flags = flags | jnp.where(flag == 1.0, 1 << k, 0)
        bits[x, pl.ds(8 * h, 8), :] = flags

    def collision(step, x, h):
        block = pl.ds(8 * h, 8)
        source = pop_ref if step == 0 else f_buf
        fluid = mask_ref[x, block, :] == 1
        near = lambda dx, dy: pot[0, x + 1 + dx, pl.ds(PAD + 8 * h + dy, 8), :]
        rates = [rate_ref[r] for r in range(19)]
        f, speed = collide([source[k, x, block, :] for k in range(19)], fluid, near, rates)
        for k in range(19):
            value = jnp.where(fluid, f[k], 0.0)
            post[step % 2, PLACE[k], x + 1, pl.ds(PAD + 8 * h, 8), :] = value
            for m in range(2):
                if k in CROSS[m] and h == leave_y[m] // 8:
                    row = leave_y[m] % 8
                    ya_send[step, m, CROSS[m].index(k), pl.ds(PAD + x, 1), :] = value[row : row + 1]
        if step == STEPS - 1:
            for c in range(3):
                vel_ref[c, x, block, :] = jnp.where(fluid, speed[c], 0.0)

    def stream(step, x, h):
        block, p = pl.ds(8 * h, 8), step % 2
        flags = bits[x, block, :]
        fluid = mask_ref[x, block, :] == 1
        density = None
        for k, (ex, ey, ez) in enumerate(VEL):
            if k == 0:
                value = post[p, PLACE[0], x + 1, pl.ds(PAD + 8 * h, 8), :]
            else:
                passed = roll_z(post[p, PLACE[k], x + 1 - ex, pl.ds(PAD + 8 * h - ey, 8), :], ez)
                bounced = post[p, PLACE[OPP[k]], x + 1, pl.ds(PAD + 8 * h, 8), :]
                value = jnp.where((flags & (1 << k)) != 0, passed, bounced)
            if step == STEPS - 1:
                out_ref[k, x, block, :] = jnp.where(fluid, value, 0.0)
            else:
                f_buf[k, x, block, :] = value
                density = value if density is None else density + value
        if step < STEPS - 1:
            dens[x, block, :] = density

    def edge_sums(step):
        p = step % 2
        for m in range(2):
            for h in range(halves):
                total = None
                for k in XK[m]:
                    _, ey, ez = VEL[k]
                    value = roll_z(
                        post[p, PLACE[k], leave_x[m] + 1, pl.ds(PAD + 8 * h - ey, 8), :], ez
                    )
                    total = value if total is None else total + value
                ox[m, pl.ds(8 * h, 8), :] = total
            total = None
            for j, k in enumerate(CROSS[m]):
                ex, _, ez = VEL[k]
                value = roll_z(ya_send[step, m, j, pl.ds(PAD - ex, nx), :], ez)
                total = value if total is None else total + value
            oy[m] = total

    def pack(step):
        one = lambda i: pl.ds(i, 1)
        for m in range(2):
            xb_send[step, m, 0] = dens[leave_x[m]]
            for n in range(2):
                xb_send[step, m, 1, one(n), :] = oy[n, one(leave_x[m]), :]
                yb_send[step, m, 1, one(n), :] = ox[n, one(leave_y[m]), :]
            for x in range(nx):
                yb_send[step, m, 0, one(x), :] = dens[x, one(leave_y[m]), :]
        for c, (sx, sy) in enumerate(CORNERS):
            mx, my = (sx + 1) // 2, (sy + 1) // 2
            cb_send[step, c, 1:2, :] = dens[leave_x[mx], one(leave_y[my]), :]
            cb_send[step, c, 2:3, :] = oy[my, one(leave_x[mx]), :]
            cb_send[step, c, 3:4, :] = ox[mx, one(leave_y[my]), :]

    def pack_corners(step):
        for c, (sx, sy) in enumerate(CORNERS):
            mx, my = (sx + 1) // 2, (sy + 1) // 2
            j = CROSS[my].index(INDEX[(sx, sy, 0)])
            cb_send[step, c, 0:1, :] = ya_send[step, my, j, pl.ds(PAD + leave_x[mx], 1), :]

    def arrive(step, k, x, block, value):
        if step == STEPS - 1:
            fluid = mask_ref[x, block, :] == 1
            out_ref[k, x, block, :] = out_ref[k, x, block, :] + jnp.where(fluid, value, 0.0)
        else:
            f_buf[k, x, block, :] = f_buf[k, x, block, :] + value

    def faces_arrive(step):
        inner = step < STEPS - 1
        for m in range(2):
            x = enter_x[m]
            for h in range(halves):
                block = pl.ds(8 * h, 8)
                total = None
                for j, k in enumerate(XK[m]):
                    _, ey, ez = VEL[k]
                    value = roll_z(xa_recv[step, m, j, pl.ds(PAD + 8 * h - ey, 8), :], ez)
                    arrive(step, k, x, block, value)
                    total = value if total is None else total + value
                if inner:
                    dens[x, block, :] = dens[x, block, :] + total
        for m in range(2):
            row = pl.ds(enter_y[m], 1)
            total = None
            for j, k in enumerate(CROSS[m]):
                ex, _, ez = VEL[k]
                value = roll_z(ya_recv[step, m, j, pl.ds(PAD - ex, nx), :], ez)
                y_tile[m, j] = value
                total = value if total is None else total + value
            y_tile[m, 5] = total
            for x in range(nx):
                for j, k in enumerate(CROSS[m]):
                    arrive(step, k, x, row, y_tile[m, j, pl.ds(x, 1), :])
                if inner:
                    dens[x, row, :] = dens[x, row, :] + y_tile[m, 5, pl.ds(x, 1), :]

    def own_potential(x, block, where):
        fluid = mask_ref[x, block, :] == 1
        value = 1.0 - jnp.exp(-dens[x, block, :])
        pot[0, x + 1, where, :] = jnp.where(fluid, value, pot[0, x + 1, where, :])

    def corners_arrive(step):
        for c, (sx, sy) in enumerate(CORNERS):
            mx, my = (sx + 1) // 2, (sy + 1) // 2
            x, y = enter_x[mx], enter_y[my]
            row = pl.ds(y, 1)
            value = cb_recv[step, c, 0:1, :]
            arrive(step, INDEX[(sx, sy, 0)], x, row, value)
            if step < STEPS - 1:
                dens[x, row, :] = dens[x, row, :] + value
                own_potential(x, row, pl.ds(PAD + y, 1))

    def ghost_potential(step):
        one = lambda i: pl.ds(i, 1)

        def put(x, where, density):
            flag = pot[1, x, where, :] == 1.0
            pot[0, x, where, :] = jnp.where(flag, 1.0 - jnp.exp(-density), pot[0, x, where, :])

        for m in range(2):
            gx_d[m] = xb_recv[step, m, 0] + ox[1 - m]
            gy_d[m] = yb_recv[step, m, 0] + oy[1 - m]
        for c, (sx, sy) in enumerate(CORNERS):
            mx, my = (sx + 1) // 2, (sy + 1) // 2
            x, y = enter_x[mx], enter_y[my]
            j = CROSS[my].index(INDEX[(-sx, sy, 0)])
            gx_d[mx, one(y), :] = gx_d[mx, one(y), :] + (
                ya_recv[step, my, j, one(PAD + x), :] + cb_recv[step, c, 2:3, :]
            )
            j = XK[mx].index(INDEX[(sx, -sy, 0)])
            gy_d[my, one(x), :] = gy_d[my, one(x), :] + (
                xa_recv[step, mx, j, one(PAD + y), :] + cb_recv[step, c, 3:4, :]
            )
            j = CROSS[1 - my].index(INDEX[(-sx, -sy, 0)])
            density = (
                cb_recv[step, c, 1:2, :] + ya_send[step, 1 - my, j, one(PAD + x), :]
            ) + (xb_recv[step, mx, 1, one(1 - my), :] + yb_recv[step, my, 1, one(1 - mx), :])
            put(ghost_x[mx], one(ghost_y[my]), density)
        for m in range(2):
            for h in range(halves):
                put(ghost_x[m], pl.ds(PAD + 8 * h, 8), gx_d[m, pl.ds(8 * h, 8), :])
            gy_d[m] = 1.0 - jnp.exp(-gy_d[m])
            for x in range(nx):
                where = one(ghost_y[m])
                flag = pot[1, x + 1, where, :] == 1.0
                pot[0, x + 1, where, :] = jnp.where(
                    flag, gy_d[m, one(x), :], pot[0, x + 1, where, :]
                )

    clear()
    for copy in fetches:
        copy.wait()
    each_block(first)
    pl.semaphore_wait(barrier, len(SENDS))
    moving = pot_copies()
    for copy in moving:
        copy.start()
    for copy in moving:
        copy.wait()
    pot_unpack()
    each_block(inflow)
    for step in range(STEPS):
        each_block(functools.partial(collision, step))
        faces = a_copies(step)
        for copy in faces:
            copy.start()
        pack_corners(step)
        others = b_copies(step)
        if step == STEPS - 1:
            for copy in others:
                copy.start()
            each_block(functools.partial(stream, step))
        else:
            each_block(functools.partial(stream, step))
            edge_sums(step)
            pack(step)
            for copy in others:
                copy.start()
        for copy in faces:
            copy.wait()
        faces_arrive(step)
        if step < STEPS - 1:
            each_block(
                lambda x, h: own_potential(x, pl.ds(8 * h, 8), pl.ds(PAD + 8 * h, 8))
            )
        for copy in others:
            copy.wait()
        corners_arrive(step)
        if step < STEPS - 1:
            ghost_potential(step)


def per_device(counts, populations, fluid_mask, wet_class, wall_potential, relax_rates):
    nx, ny, nz = fluid_mask.shape
    vmem = pl.BlockSpec(memory_space=pltpu.VMEM)
    hbm = pl.BlockSpec(memory_space=pltpu.HBM)
    f32 = jnp.float32
    padded = (nx + 2, ny + 2 * PAD, nz)
    return pl.pallas_call(
        functools.partial(kernel, counts),
        out_shape=(
            jax.ShapeDtypeStruct((19, nx, ny, nz), f32),
            jax.ShapeDtypeStruct((3, nx, ny, nz), f32),
        ),
        in_specs=[hbm] * 5,
        out_specs=(vmem, vmem),
        scratch_shapes=[
            pltpu.VMEM(populations.shape, f32),
            pltpu.VMEM(fluid_mask.shape, jnp.int32),
            pltpu.VMEM(wet_class.shape, jnp.int32),
            pltpu.SMEM(wall_potential.shape, f32),
            pltpu.SMEM(relax_rates.shape, f32),
            pltpu.VMEM((2,) + padded, f32),
            pltpu.VMEM((19, nx, ny, nz), f32),
            pltpu.VMEM((nx, ny, nz), f32),
            pltpu.VMEM((nx, ny, nz), jnp.int32),
            pltpu.VMEM((2, 19) + padded, f32),
            pltpu.VMEM((2, 2, nx, nz), f32),
            pltpu.VMEM((2, 2, nx, nz), f32),
            pltpu.VMEM((4, 2, nx, nz), f32),
            pltpu.VMEM((STEPS, 2, 5, ny + 2 * PAD, nz), f32),
            pltpu.VMEM((STEPS, 2, 5, nx + 2 * PAD, nz), f32),
            pltpu.VMEM((STEPS, 2, 5, nx + 2 * PAD, nz), f32),
            pltpu.VMEM((STEPS, 2, 2, ny, nz), f32),
            pltpu.VMEM((STEPS, 2, 2, ny, nz), f32),
            pltpu.VMEM((STEPS, 2, 2, nx, nz), f32),
            pltpu.VMEM((STEPS, 2, 2, nx, nz), f32),
            pltpu.VMEM((STEPS, 4, 8, nz), f32),
            pltpu.VMEM((STEPS, 4, 8, nz), f32),
            pltpu.VMEM((2, ny, nz), f32),
            pltpu.VMEM((2, nx, nz), f32),
            pltpu.VMEM((2, ny, nz), f32),
            pltpu.VMEM((2, nx, nz), f32),
            pltpu.VMEM((2, 6, nx, nz), f32),
            pltpu.SemaphoreType.DMA((5,)),
            pltpu.SemaphoreType.DMA((8,)),
            pltpu.SemaphoreType.DMA((8,)),
            pltpu.SemaphoreType.DMA((STEPS, 12)),
            pltpu.SemaphoreType.DMA((STEPS, 12)),
        ],
        compiler_params=pltpu.CompilerParams(
            collective_id=0, has_side_effects=True, vmem_limit_bytes=48 * 1024 * 1024
        ),
    )(populations, fluid_mask, wet_class, wall_potential, relax_rates)


def solution(mesh):
    counts = (mesh.shape["gx"], mesh.shape["gy"])
    return jax.shard_map(
        functools.partial(per_device, counts),
        mesh=mesh,
        in_specs=(
            P(None, ("groups", "gx"), "gy", None),
            P(("groups", "gx"), "gy", None),
            P(("groups", "gx"), "gy", None),
            P("groups"),
            P(),
        ),
        out_specs=(P(None, ("groups", "gx"), "gy", None), P(None, ("groups", "gx"), "gy", None)),
        check_vma=False,
    )
```

```python
import functools

import jax
import jax.numpy as jnp
from jax import lax
from jax.experimental import pallas as pl
from jax.experimental.pallas import tpu as pltpu
from jax.sharding import PartitionSpec as P

WET_CLASSES = 4
STEPS = 4
COUPLING = 2.5
PAD = 8
VEL = [
    (0, 0, 0),
    (1, 0, 0),
    (-1, 0, 0),
    (0, 1, 0),
    (0, -1, 0),
    (0, 0, 1),
    (0, 0, -1),
    (1, 1, 0),
    (-1, -1, 0),
    (1, -1, 0),
    (-1, 1, 0),
    (1, 0, 1),
    (-1, 0, -1),
    (1, 0, -1),
    (-1, 0, 1),
    (0, 1, 1),
    (0, -1, -1),
    (0, 1, -1),
    (0, -1, 1),
]
INDEX = {v: k for k, v in enumerate(VEL)}
OPP = [INDEX[(-a, -b, -c)] for a, b, c in VEL]
ORDER = (
    [k for k in range(19) if VEL[k][0] == 1]
    + [k for k in range(19) if VEL[k][0] == -1]
    + [k for k in range(19) if VEL[k][0] == 0]
)
PLACE = [ORDER.index(k) for k in range(19)]
CROSS = [[k for k in range(19) if VEL[k][1] == s] for s in (-1, 1)]
CORNERS = [(1, 1), (1, -1), (-1, 1), (-1, -1)]
SENDS = [(1, 0), (-1, 0), (0, 1), (0, -1)] + CORNERS


def roll_z(value, step):
    if step == 0:
        return value
    return pltpu.roll(value, step % value.shape[-1], axis=value.ndim - 1)


def to_moments(f):
    g = lambda *v: f[INDEX[v]]
    m = {}

    def plane(pp, mm, pm, mp):
        a, b, c, d = pp + mm, pm + mp, pp - mm, pm - mp
        return a + b, a - b, c + d, c - d

    m["xxyy"], m["xy"], m["xyy"], m["yxx"] = plane(
        g(1, 1, 0), g(-1, -1, 0), g(1, -1, 0), g(-1, 1, 0)
    )
    m["xxzz"], m["xz"], m["xzz"], m["zxx"] = plane(
        g(1, 0, 1), g(-1, 0, -1), g(1, 0, -1), g(-1, 0, 1)
    )
    m["yyzz"], m["yz"], m["yzz"], m["zyy"] = plane(
        g(0, 1, 1), g(0, -1, -1), g(0, 1, -1), g(0, -1, 1)
    )
    sx, dx = f[1] + f[2], f[1] - f[2]
    sy, dy = f[3] + f[4], f[3] - f[4]
    sz, dz = f[5] + f[6], f[5] - f[6]
    m["xx"] = sx + (m["xxyy"] + m["xxzz"])
    m["yy"] = sy + (m["xxyy"] + m["yyzz"])
    m["zz"] = sz + (m["xxzz"] + m["yyzz"])
    m["x"] = dx + (m["xyy"] + m["xzz"])
    m["y"] = dy + (m["yxx"] + m["yzz"])
    m["z"] = dz + (m["zxx"] + m["zyy"])
    m["1"] = ((f[0] + sx) + (sy + sz)) + ((m["xxyy"] + m["xxzz"]) + m["yyzz"])
    return m


def from_moments(m):
    f = [None] * 19

    def plane(even, cross, first, second, v):
        a, b = 0.25 * (even + cross), 0.25 * (even - cross)
        c, d = 0.25 * (first + second), 0.25 * (first - second)
        values = (a + c, a - c, b + d, b - d)
        for velocity, value in zip(v, values):
            f[INDEX[velocity]] = value

    plane(m["xxyy"], m["xy"], m["xyy"], m["yxx"], [(1, 1, 0), (-1, -1, 0), (1, -1, 0), (-1, 1, 0)])
    plane(m["xxzz"], m["xz"], m["xzz"], m["zxx"], [(1, 0, 1), (-1, 0, -1), (1, 0, -1), (-1, 0, 1)])
    plane(m["yyzz"], m["yz"], m["yzz"], m["zyy"], [(0, 1, 1), (0, -1, -1), (0, 1, -1), (0, -1, 1)])
    sx = m["xx"] - (m["xxyy"] + m["xxzz"])
    sy = m["yy"] - (m["xxyy"] + m["yyzz"])
    sz = m["zz"] - (m["xxzz"] + m["yyzz"])
    dx = m["x"] - (m["xyy"] + m["xzz"])
    dy = m["y"] - (m["yxx"] + m["yzz"])
    dz = m["z"] - (m["zxx"] + m["zyy"])
    f[1], f[2] = 0.5 * (sx + dx), 0.5 * (sx - dx)
    f[3], f[4] = 0.5 * (sy + dy), 0.5 * (sy - dy)
    f[5], f[6] = 0.5 * (sz + dz), 0.5 * (sz - dz)
    f[0] = (m["1"] - (sx + sy)) - (sz + ((m["xxyy"] + m["xxzz"]) + m["yyzz"]))
    return f


NAMES = [
    "1", "x", "y", "z", "xy", "xz", "yz", "xx", "yy", "zz",
    "xyy", "xzz", "yxx", "yzz", "zxx", "zyy", "xxyy", "xxzz", "yyzz",
]


def collide(f, fluid, near, rates):
    third = 1.0 / 3.0
    m = to_moments(f)
    here = near(0, 0)
    xp, xm, yp, ym = near(1, 0), near(-1, 0), near(0, 1), near(0, -1)
    dx, dy = xp - xm, yp - ym
    ring = (2.0 * here + (xp + xm)) + (yp + ym)
    pp, pm, mp, mm = near(1, 1), near(1, -1), near(-1, 1), near(-1, -1)
    a, b = pp - mm, pm - mp
    scale = (COUPLING / 36.0) * here
    fx = scale * ((2.0 * dx + (a + b)) + (roll_z(dx, 1) + roll_z(dx, -1)))
    fy = scale * ((2.0 * dy + (a - b)) + (roll_z(dy, 1) + roll_z(dy, -1)))
    fz = scale * (roll_z(ring, -1) - roll_z(ring, 1))
    rho = jnp.where(fluid, m["1"], 1.0)
    inv = 1.0 / rho
    ux, uy, uz = ((m[n] + 0.5 * v) * inv for n, v in (("x", fx), ("y", fy), ("z", fz)))
    jx, jy, jz = rho * ux, rho * uy, rho * uz
    qx, qy, qz = jx * ux, jy * uy, jz * uz
    wx, wy, wz = ux * fx, uy * fy, uz * fz
    rho3, rho9 = rho * third, rho * (1.0 / 9.0)
    hx, hy, hz = (0.5 * q for q in (qx, qy, qz))
    hsum = rho9 - third * (hx + hy + hz)
    wsum = third * (wx + wy + wz)
    equil = {
        "1": rho, "x": jx, "y": jy, "z": jz,
        "xy": jx * uy, "xz": jx * uz, "yz": jy * uz,
        "xx": rho3 + qx, "yy": rho3 + qy, "zz": rho3 + qz,
        "xyy": jx * third, "yxx": jy * third, "zxx": jz * third,
        "xxyy": hsum + (hx + hy), "xxzz": hsum + (hx + hz), "yyzz": hsum + (hy + hz),
    }
    source = {
        "1": None, "x": fx, "y": fy, "z": fz,
        "xy": fx * uy + fy * ux, "xz": fx * uz + fz * ux, "yz": fy * uz + fz * uy,
        "xx": 2.0 * wx, "yy": 2.0 * wy, "zz": 2.0 * wz,
        "xyy": fx * third, "yxx": fy * third, "zxx": fz * third,
        "xxyy": (wx + wy) - wsum, "xxzz": (wx + wz) - wsum, "yyzz": (wy + wz) - wsum,
    }
    for table in (equil, source):
        table["xzz"], table["yzz"], table["zyy"] = table["xyy"], table["yxx"], table["zxx"]
    after = {}
    for row, name in enumerate(NAMES):
        rate = rates[row]
        if source[name] is None:
            after[name] = m[name] + rate * (equil[name] - m[name])
        else:
            after[name] = (m[name] + source[name]) + rate * (
                (equil[name] - m[name]) - 0.5 * source[name]
            )
    return from_moments(after), (ux, uy, uz)


def kernel(
    counts, pop_hbm, mask_hbm, wet_hbm, wall_hbm, rate_hbm, out_hbm, vel_hbm,
    out_ref, vel_ref, pop_ref, mask_ref, wet_ref, wall_ref, rate_ref,
    pot, f_buf, dens, bits, post, pot_ysend, pot_yrecv, pot_crecv,
    xa_recv, ya_send, ya_recv, xb_send, xb_recv, yb_send, yb_recv, cb_send, cb_recv,
    ox, oy, gx_d, gy_d, y_tile,
    in_sem, out_sem, pot_send_sem, pot_recv_sem, send_sem, recv_sem,
):
    nx, ny, nz = mask_ref.shape
    halves = ny // 8
    top = PAD + ny
    gx, gy = lax.axis_index("gx"), lax.axis_index("gy")
    SIGN = (-1, 1)
    leave_x, leave_y = (0, nx - 1), (0, ny - 1)
    enter_x, enter_y = (nx - 1, 0), (ny - 1, 0)
    ghost_x, ghost_y = (nx + 1, 0), (top, PAD - 1)
    XK = [ORDER[5:10], ORDER[0:5]]

    fetches = [
        pltpu.make_async_copy(a, b, in_sem.at[i])
        for i, (a, b) in enumerate(
            [
                (pop_hbm, pop_ref),
                (mask_hbm, mask_ref),
                (wet_hbm, wet_ref),
                (wall_hbm, wall_ref),
                (rate_hbm, rate_ref),
            ]
        )
    ]
    for copy in fetches:
        copy.start()

    def neighbour(d):
        return {
            "gx": lax.rem(gx + d[0] + counts[0], counts[0]),
            "gy": lax.rem(gy + d[1] + counts[1], counts[1]),
        }

    barrier = pltpu.get_barrier_semaphore()
    for d in SENDS:
        pl.semaphore_signal(
            barrier, inc=1, device_id=neighbour(d), device_id_type=pl.DeviceIdType.MESH
        )

    def remote(src, dst, sent, received, d):
        return pltpu.make_async_remote_copy(
            src_ref=src,
            dst_ref=dst,
            send_sem=sent,
            recv_sem=received,
            device_id=neighbour(d),
            device_id_type=pl.DeviceIdType.MESH,
        )

    rows = pl.ds(PAD, ny)
    xrows = pl.ds(PAD, nx)

    def pot_copies():
        pairs = {
            (1, 0): (pot.at[:, nx, rows], pot.at[:, 0, rows]),
            (-1, 0): (pot.at[:, 1, rows], pot.at[:, nx + 1, rows]),
        }
        for side, s in enumerate(SIGN):
            pairs[(0, s)] = (pot_ysend.at[side], pot_yrecv.at[side])
            for c, d in enumerate(CORNERS):
                if d[1] == s:
                    pairs[d] = (pot_ysend.at[side], pot_crecv.at[c])
        return [
            remote(*pairs[d], pot_send_sem.at[i], pot_recv_sem.at[i], d)
            for i, d in enumerate(SENDS)
        ]

    def a_copies(step, dim):
        p = step % 2
        made = []
        for m, s in enumerate(SIGN):
            if dim == "x":
                part = pl.ds(5 * (1 - m), 5)
                src = post.at[p, part, leave_x[m] + 1, rows]
                dst, i, d = xa_recv.at[step, m, :, rows], m, (s, 0)
            else:
                src = ya_send.at[step, m, :, xrows]
                dst, i, d = ya_recv.at[step, m, :, xrows], 2 + m, (0, s)
            made.append(remote(src, dst, send_sem.at[step, i], recv_sem.at[step, i], d))
        return made

    def b_copies(step, dim):
        made = []
        if dim == "corner":
            for c, d in enumerate(CORNERS):
                src, dst, i = cb_send.at[step, c], cb_recv.at[step, c], 8 + c
                made.append(remote(src, dst, send_sem.at[step, i], recv_sem.at[step, i], d))
        elif step < STEPS - 1:
            for m, s in enumerate(SIGN):
                if dim == "x":
                    src, dst, i, d = xb_send.at[step, m], xb_recv.at[step, m], 4 + m, (s, 0)
                else:
                    src, dst, i, d = yb_send.at[step, m], yb_recv.at[step, m], 6 + m, (0, s)
                made.append(remote(src, dst, send_sem.at[step, i], recv_sem.at[step, i], d))
        return made

    def clear():
        tile = jnp.zeros((8, nz), jnp.float32)
        for p in range(2):
            for m in range(2):
                for k in XK[m]:
                    for r in range((ny + 2 * PAD) // 8):
                        post[p, PLACE[k], ghost_x[m], pl.ds(8 * r, 8), :] = tile
                for k in CROSS[m]:
                    for x in range(nx):
                        post[p, PLACE[k], x + 1, pl.ds((top, 0)[m], 8), :] = tile
        for step in range(STEPS):
            for m in range(2):
                for j in range(5):
                    for r in (0, top):
                        xa_recv[step, m, j, pl.ds(r, 8), :] = tile
                    ya_send[step, m, j] = jnp.zeros((nx + 2 * PAD, nz), jnp.float32)
                    for r in (0, PAD + nx):
                        ya_recv[step, m, j, pl.ds(r, 8), :] = tile
                xb_send[step, m, pl.ds(ny, 8), :] = tile
                yb_send[step, m, 1] = jnp.zeros((nx, nz), jnp.float32)
            for c in range(4):
                cb_send[step, c] = tile

    def pot_unpack():
        for part in range(2):
            for m in range(2):
                for x in range(nx):
                    pot[part, x + 1, pl.ds(ghost_y[m], 1), :] = pot_yrecv[m, part, pl.ds(x, 1), :]
            for c, (sx, sy) in enumerate(CORNERS):
                mx, my = (sx + 1) // 2, (sy + 1) // 2
                pot[part, ghost_x[mx], pl.ds(ghost_y[my], 1), :] = pot_crecv[
                    c, part, pl.ds(leave_x[mx], 1), :
                ]

    def each_block(body, start=0, count=nx, stride=1):
        def plane(i, carry):
            for h in range(halves):
                body(start + i * stride, h)
            return carry

        lax.fori_loop(0, count, plane, 0)

    def first(x, h):
        block = pl.ds(8 * h, 8)
        fluid = mask_ref[x, block, :] == 1
        density = pop_ref[0, x, block, :]
        for k in range(1, 19):
            density = density + pop_ref[k, x, block, :]
        wet = wet_ref[x, block, :]
        wall = jnp.zeros_like(density)
        for c in range(WET_CLASSES):
            wall = wall + jnp.where(wet == c, wall_ref[c], 0.0)
        safe = jnp.where(fluid, density, 1.0)
        flag = jnp.where(fluid, 1.0, 0.0)
        for part, value in enumerate((jnp.where(fluid, 1.0 - jnp.exp(-safe), wall), flag)):
            pot[part, x + 1, pl.ds(PAD + 8 * h, 8), :] = value
            for m in range(2):
                if h == leave_y[m] // 8:
                    row = leave_y[m] % 8
                    pot_ysend[m, part, pl.ds(x, 1), :] = value[row : row + 1]

    def inflow(x, h):
        flags = jnp.zeros((8, nz), jnp.int32)
        for k, (ex, ey, ez) in enumerate(VEL):
            if k > 0:
                flag = roll_z(pot[1, x + 1 - ex, pl.ds(PAD + 8 * h - ey, 8), :], ez)
                flags = flags | jnp.where(flag == 1.0, 1 << k, 0)
        bits[x, pl.ds(8 * h, 8), :] = flags

    def collision(step, x, h):
        block = pl.ds(8 * h, 8)
        source = pop_ref if step == 0 else f_buf
        fluid = mask_ref[x, block, :] == 1
        near = lambda dx, dy: pot[0, x + 1 + dx, pl.ds(PAD + 8 * h + dy, 8), :]
        rates = [rate_ref[r] for r in range(19)]
        f, speed = collide([source[k, x, block, :] for k in range(19)], fluid, near, rates)
        for k in range(19):
            value = jnp.where(fluid, f[k], 0.0)
            post[step % 2, PLACE[k], x + 1, pl.ds(PAD + 8 * h, 8), :] = value
            for m in range(2):
                if k in CROSS[m] and h == leave_y[m] // 8:
                    row = leave_y[m] % 8
                    ya_send[step, m, CROSS[m].index(k), pl.ds(PAD + x, 1), :] = value[row : row + 1]
        if step == STEPS - 1:
            for c in range(3):
                vel_ref[c, x, block, :] = jnp.where(fluid, speed[c], 0.0)

    def stream(step, x, h):
        block, p = pl.ds(8 * h, 8), step % 2
        flags = bits[x, block, :]
        fluid = mask_ref[x, block, :] == 1
        density = None
        for k, (ex, ey, ez) in enumerate(VEL):
            if k == 0:
                value = post[p, PLACE[0], x + 1, pl.ds(PAD + 8 * h, 8), :]
            else:
                passed = roll_z(post[p, PLACE[k], x + 1 - ex, pl.ds(PAD + 8 * h - ey, 8), :], ez)
                bounced = post[p, PLACE[OPP[k]], x + 1, pl.ds(PAD + 8 * h, 8), :]
                value = jnp.where((flags & (1 << k)) != 0, passed, bounced)
            if step == STEPS - 1:
                out_ref[k, x, block, :] = jnp.where(fluid, value, 0.0)
            else:
                f_buf[k, x, block, :] = value
                density = value if density is None else density + value
        if step < STEPS - 1:
            dens[x, block, :] = density

    def x_sums(step):
        for m in range(2):
            for h in range(halves):
                total = None
                for k in XK[m]:
                    _, ey, ez = VEL[k]
                    value = roll_z(
                        post[step % 2, PLACE[k], leave_x[m] + 1, pl.ds(PAD + 8 * h - ey, 8), :], ez
                    )
                    total = value if total is None else total + value
                ox[m, pl.ds(8 * h, 8), :] = total

    def y_sums(step):
        for m in range(2):
            total = None
            for j, k in enumerate(CROSS[m]):
                ex, _, ez = VEL[k]
                value = roll_z(ya_send[step, m, j, pl.ds(PAD - ex, nx), :], ez)
                total = value if total is None else total + value
            oy[m] = total

    one = lambda i: pl.ds(i, 1)

    def pack_x(step):
        for m in range(2):
            xb_send[step, m, pl.ds(0, ny), :] = dens[leave_x[m]]
            for n in range(2):
                xb_send[step, m, one(ny + n), :] = oy[n, one(leave_x[m]), :]
        for c, (sx, sy) in enumerate(CORNERS):
            mx, my = (sx + 1) // 2, (sy + 1) // 2
            cb_send[step, c, 1:2, :] = dens[leave_x[mx], one(leave_y[my]), :]
            cb_send[step, c, 2:3, :] = oy[my, one(leave_x[mx]), :]
            cb_send[step, c, 3:4, :] = ox[mx, one(leave_y[my]), :]

    def pack_y(step):
        for m in range(2):
            for n in range(2):
                yb_send[step, m, 1, one(n), :] = ox[n, one(leave_y[m]), :]
            for x in range(nx):
                yb_send[step, m, 0, one(x), :] = dens[x, one(leave_y[m]), :]

    def pack_corners(step):
        for c, (sx, sy) in enumerate(CORNERS):
            mx, my = (sx + 1) // 2, (sy + 1) // 2
            j = CROSS[my].index(INDEX[(sx, sy, 0)])
            cb_send[step, c, 0:1, :] = ya_send[step, my, j, pl.ds(PAD + leave_x[mx], 1), :]

    def arrive(step, k, x, block, value):
        if step == STEPS - 1:
            fluid = mask_ref[x, block, :] == 1
            out_ref[k, x, block, :] = out_ref[k, x, block, :] + jnp.where(fluid, value, 0.0)
        else:
            f_buf[k, x, block, :] = f_buf[k, x, block, :] + value

    def x_arrive(step):
        for m in range(2):
            x = enter_x[m]
            for h in range(halves):
                block = pl.ds(8 * h, 8)
                total = None
                for j, k in enumerate(XK[m]):
                    _, ey, ez = VEL[k]
                    value = roll_z(xa_recv[step, m, j, pl.ds(PAD + 8 * h - ey, 8), :], ez)
                    arrive(step, k, x, block, value)
                    total = value if total is None else total + value
                if step < STEPS - 1:
                    dens[x, block, :] = dens[x, block, :] + total

    def y_arrive(step):
        for m in range(2):
            row = pl.ds(enter_y[m], 1)
            total = None
            for j, k in enumerate(CROSS[m]):
                ex, _, ez = VEL[k]
                value = roll_z(ya_recv[step, m, j, pl.ds(PAD - ex, nx), :], ez)
                y_tile[m, j] = value
                total = value if total is None else total + value
            y_tile[m, 5] = total
            for x in range(nx):
                for j, k in enumerate(CROSS[m]):
                    arrive(step, k, x, row, y_tile[m, j, pl.ds(x, 1), :])
                if step < STEPS - 1:
                    dens[x, row, :] = dens[x, row, :] + y_tile[m, 5, pl.ds(x, 1), :]

    def own_potential(x, h):
        block, where = pl.ds(8 * h, 8), pl.ds(PAD + 8 * h, 8)
        fluid = mask_ref[x, block, :] == 1
        value = 1.0 - jnp.exp(-dens[x, block, :])
        pot[0, x + 1, where, :] = jnp.where(fluid, value, pot[0, x + 1, where, :])

    def corners_arrive(step):
        for c, (sx, sy) in enumerate(CORNERS):
            mx, my = (sx + 1) // 2, (sy + 1) // 2
            x, y = enter_x[mx], enter_y[my]
            row = pl.ds(y, 1)
            value = cb_recv[step, c, 0:1, :]
            arrive(step, INDEX[(sx, sy, 0)], x, row, value)
            if step < STEPS - 1:
                dens[x, row, :] = dens[x, row, :] + value

    def ghost_potential(step):
        def put(x, where, density):
            flag = pot[1, x, where, :] == 1.0
            pot[0, x, where, :] = jnp.where(flag, 1.0 - jnp.exp(-density), pot[0, x, where, :])

        for m in range(2):
            gx_d[m] = xb_recv[step, m, pl.ds(0, ny), :] + ox[1 - m]
            gy_d[m] = yb_recv[step, m, 0] + oy[1 - m]
        for c, (sx, sy) in enumerate(CORNERS):
            mx, my = (sx + 1) // 2, (sy + 1) // 2
            x, y = enter_x[mx], enter_y[my]
            j = CROSS[my].index(INDEX[(-sx, sy, 0)])
            gx_d[mx, one(y), :] = gx_d[mx, one(y), :] + (
                ya_recv[step, my, j, one(PAD + x), :] + cb_recv[step, c, 2:3, :]
            )
            j = XK[mx].index(INDEX[(sx, -sy, 0)])
            gy_d[my, one(x), :] = gy_d[my, one(x), :] + (
                xa_recv[step, mx, j, one(PAD + y), :] + cb_recv[step, c, 3:4, :]
            )
            j = CROSS[1 - my].index(INDEX[(-sx, -sy, 0)])
            density = (
                cb_recv[step, c, 1:2, :] + ya_send[step, 1 - my, j, one(PAD + x), :]
            ) + (xb_recv[step, mx, one(ny + 1 - my), :] + yb_recv[step, my, 1, one(1 - mx), :])
            put(ghost_x[mx], one(ghost_y[my]), density)
        for m in range(2):
            for h in range(halves):
                put(ghost_x[m], pl.ds(PAD + 8 * h, 8), gx_d[m, pl.ds(8 * h, 8), :])
            gy_d[m] = 1.0 - jnp.exp(-gy_d[m])
            for x in range(nx):
                where = one(ghost_y[m])
                flag = pot[1, x + 1, where, :] == 1.0
                pot[0, x + 1, where, :] = jnp.where(
                    flag, gy_d[m, one(x), :], pot[0, x + 1, where, :]
                )

    clear()
    for copy in fetches:
        copy.wait()
    each_block(first)
    pl.semaphore_wait(barrier, len(SENDS))
    moving = pot_copies()
    for copy in moving:
        copy.start()
    for copy in moving:
        copy.wait()
    pot_unpack()
    each_block(inflow)

    def start(group):
        for copy in group:
            copy.start()
        return group

    def finish(group):
        for copy in group:
            copy.wait()

    EDGE, NEXT, INNER = (0, 2, nx - 1), (1, 2, nx - 3), (2, nx - 4, 1)
    WITHIN = (1, nx - 2, 1)
    for step in range(STEPS):
        final = step == STEPS - 1
        hit = functools.partial(collision, step)
        move = functools.partial(stream, step)
        each_block(hit, *EDGE)
        x_moving = start(a_copies(step, "x"))
        pack_corners(step)
        if not final:
            each_block(hit, *NEXT)
            each_block(move, *EDGE)
            x_sums(step)
            y_sums(step)
            pack_x(step)
        x_moving += start(b_copies(step, "x") + b_copies(step, "corner"))
        if final:
            each_block(hit, *NEXT)
        each_block(hit, *INNER)
        y_moving = start(a_copies(step, "y"))
        if final:
            leaving = [pltpu.make_async_copy(vel_ref, vel_hbm, out_sem.at[0])]
            leaving[0].start()
            each_block(move)
        else:
            each_block(move, *WITHIN)
            y_sums(step)
            pack_y(step)
            y_moving += start(b_copies(step, "y"))
        finish(y_moving)
        y_arrive(step)
        if final:
            for i, (x, count) in enumerate([(1, nx - 2), (0, 1), (nx - 1, 1)]):
                where = pl.ds(x, count)
                leaving.append(
                    pltpu.make_async_copy(
                        out_ref.at[:, where], out_hbm.at[:, where], out_sem.at[1 + i]
                    )
                )
            leaving[1].start()
        else:
            each_block(own_potential, *WITHIN)
        finish(x_moving)
        x_arrive(step)
        corners_arrive(step)
        if final:
            leaving[2].start()
            leaving[3].start()
            finish(leaving)
        else:
            each_block(own_potential, *EDGE)
            ghost_potential(step)


def per_device(counts, populations, fluid_mask, wet_class, wall_potential, relax_rates):
    nx, ny, nz = fluid_mask.shape
    hbm = pl.BlockSpec(memory_space=pltpu.HBM)
    f32 = jnp.float32
    padded = (nx + 2, ny + 2 * PAD, nz)
    return pl.pallas_call(
        functools.partial(kernel, counts),
        out_shape=(
            jax.ShapeDtypeStruct((19, nx, ny, nz), f32),
            jax.ShapeDtypeStruct((3, nx, ny, nz), f32),
        ),
        in_specs=[hbm] * 5,
        out_specs=(hbm, hbm),
        scratch_shapes=[
            pltpu.VMEM((19, nx, ny, nz), f32),
            pltpu.VMEM((3, nx, ny, nz), f32),
            pltpu.VMEM(populations.shape, f32),
            pltpu.VMEM(fluid_mask.shape, jnp.int32),
            pltpu.VMEM(wet_class.shape, jnp.int32),
            pltpu.SMEM(wall_potential.shape, f32),
            pltpu.SMEM(relax_rates.shape, f32),
            pltpu.VMEM((2,) + padded, f32),
            pltpu.VMEM((19, nx, ny, nz), f32),
            pltpu.VMEM((nx, ny, nz), f32),
            pltpu.VMEM((nx, ny, nz), jnp.int32),
            pltpu.VMEM((2, 19) + padded, f32),
            pltpu.VMEM((2, 2, nx, nz), f32),
            pltpu.VMEM((2, 2, nx, nz), f32),
            pltpu.VMEM((4, 2, nx, nz), f32),
            pltpu.VMEM((STEPS, 2, 5, ny + 2 * PAD, nz), f32),
            pltpu.VMEM((STEPS, 2, 5, nx + 2 * PAD, nz), f32),
            pltpu.VMEM((STEPS, 2, 5, nx + 2 * PAD, nz), f32),
            pltpu.VMEM((STEPS, 2, ny + 8, nz), f32),
            pltpu.VMEM((STEPS, 2, ny + 8, nz), f32),
            pltpu.VMEM((STEPS, 2, 2, nx, nz), f32),
            pltpu.VMEM((STEPS, 2, 2, nx, nz), f32),
            pltpu.VMEM((STEPS, 4, 8, nz), f32),
            pltpu.VMEM((STEPS, 4, 8, nz), f32),
            pltpu.VMEM((2, ny, nz), f32),
            pltpu.VMEM((2, nx, nz), f32),
            pltpu.VMEM((2, ny, nz), f32),
            pltpu.VMEM((2, nx, nz), f32),
            pltpu.VMEM((2, 6, nx, nz), f32),
            pltpu.SemaphoreType.DMA((5,)),
            pltpu.SemaphoreType.DMA((4,)),
            pltpu.SemaphoreType.DMA((8,)),
            pltpu.SemaphoreType.DMA((8,)),
            pltpu.SemaphoreType.DMA((STEPS, 12)),
            pltpu.SemaphoreType.DMA((STEPS, 12)),
        ],
        compiler_params=pltpu.CompilerParams(
            collective_id=0, has_side_effects=True, vmem_limit_bytes=60 * 1024 * 1024
        ),
    )(populations, fluid_mask, wet_class, wall_potential, relax_rates)


def solution(mesh):
    counts = (mesh.shape["gx"], mesh.shape["gy"])
    return jax.shard_map(
        functools.partial(per_device, counts),
        mesh=mesh,
        in_specs=(
            P(None, ("groups", "gx"), "gy", None),
            P(("groups", "gx"), "gy", None),
            P(("groups", "gx"), "gy", None),
            P("groups"),
            P(),
        ),
        out_specs=(P(None, ("groups", "gx"), "gy", None), P(None, ("groups", "gx"), "gy", None)),
        check_vma=False,
    )
```

```python
import functools

import jax
import jax.numpy as jnp
from jax import lax
from jax.experimental import pallas as pl
from jax.experimental.pallas import tpu as pltpu
from jax.sharding import PartitionSpec as P

WET_CLASSES = 4
STEPS = 4
COUPLING = 2.5
PAD = 8
VEL = [
    (0, 0, 0),
    (1, 0, 0),
    (-1, 0, 0),
    (0, 1, 0),
    (0, -1, 0),
    (0, 0, 1),
    (0, 0, -1),
    (1, 1, 0),
    (-1, -1, 0),
    (1, -1, 0),
    (-1, 1, 0),
    (1, 0, 1),
    (-1, 0, -1),
    (1, 0, -1),
    (-1, 0, 1),
    (0, 1, 1),
    (0, -1, -1),
    (0, 1, -1),
    (0, -1, 1),
]
INDEX = {v: k for k, v in enumerate(VEL)}
OPP = [INDEX[(-a, -b, -c)] for a, b, c in VEL]
ORDER = (
    [k for k in range(19) if VEL[k][0] == 1]
    + [k for k in range(19) if VEL[k][0] == -1]
    + [k for k in range(19) if VEL[k][0] == 0]
)
PLACE = [ORDER.index(k) for k in range(19)]
CROSS = [[k for k in range(19) if VEL[k][1] == s] for s in (-1, 1)]
CORNERS = [(1, 1), (1, -1), (-1, 1), (-1, -1)]
SENDS = [(1, 0), (-1, 0), (0, 1), (0, -1)] + CORNERS


def roll_z(value, step):
    if step == 0:
        return value
    return pltpu.roll(value, step % value.shape[-1], axis=value.ndim - 1)


def to_moments(f):
    g = lambda *v: f[INDEX[v]]
    m = {}

    def plane(pp, mm, pm, mp):
        a, b, c, d = pp + mm, pm + mp, pp - mm, pm - mp
        return a + b, a - b, c + d, c - d

    m["xxyy"], m["xy"], m["xyy"], m["yxx"] = plane(
        g(1, 1, 0), g(-1, -1, 0), g(1, -1, 0), g(-1, 1, 0)
    )
    m["xxzz"], m["xz"], m["xzz"], m["zxx"] = plane(
        g(1, 0, 1), g(-1, 0, -1), g(1, 0, -1), g(-1, 0, 1)
    )
    m["yyzz"], m["yz"], m["yzz"], m["zyy"] = plane(
        g(0, 1, 1), g(0, -1, -1), g(0, 1, -1), g(0, -1, 1)
    )
    sx, dx = f[1] + f[2], f[1] - f[2]
    sy, dy = f[3] + f[4], f[3] - f[4]
    sz, dz = f[5] + f[6], f[5] - f[6]
    m["xx"] = sx + (m["xxyy"] + m["xxzz"])
    m["yy"] = sy + (m["xxyy"] + m["yyzz"])
    m["zz"] = sz + (m["xxzz"] + m["yyzz"])
    m["x"] = dx + (m["xyy"] + m["xzz"])
    m["y"] = dy + (m["yxx"] + m["yzz"])
    m["z"] = dz + (m["zxx"] + m["zyy"])
    m["1"] = ((f[0] + sx) + (sy + sz)) + ((m["xxyy"] + m["xxzz"]) + m["yyzz"])
    return m


def from_moments(m):
    f = [None] * 19

    def plane(even, cross, first, second, v):
        a, b = 0.25 * (even + cross), 0.25 * (even - cross)
        c, d = 0.25 * (first + second), 0.25 * (first - second)
        values = (a + c, a - c, b + d, b - d)
        for velocity, value in zip(v, values):
            f[INDEX[velocity]] = value

    plane(m["xxyy"], m["xy"], m["xyy"], m["yxx"], [(1, 1, 0), (-1, -1, 0), (1, -1, 0), (-1, 1, 0)])
    plane(m["xxzz"], m["xz"], m["xzz"], m["zxx"], [(1, 0, 1), (-1, 0, -1), (1, 0, -1), (-1, 0, 1)])
    plane(m["yyzz"], m["yz"], m["yzz"], m["zyy"], [(0, 1, 1), (0, -1, -1), (0, 1, -1), (0, -1, 1)])
    sx = m["xx"] - (m["xxyy"] + m["xxzz"])
    sy = m["yy"] - (m["xxyy"] + m["yyzz"])
    sz = m["zz"] - (m["xxzz"] + m["yyzz"])
    dx = m["x"] - (m["xyy"] + m["xzz"])
    dy = m["y"] - (m["yxx"] + m["yzz"])
    dz = m["z"] - (m["zxx"] + m["zyy"])
    f[1], f[2] = 0.5 * (sx + dx), 0.5 * (sx - dx)
    f[3], f[4] = 0.5 * (sy + dy), 0.5 * (sy - dy)
    f[5], f[6] = 0.5 * (sz + dz), 0.5 * (sz - dz)
    f[0] = (m["1"] - (sx + sy)) - (sz + ((m["xxyy"] + m["xxzz"]) + m["yyzz"]))
    return f


NAMES = [
    "1", "x", "y", "z", "xy", "xz", "yz", "xx", "yy", "zz",
    "xyy", "xzz", "yxx", "yzz", "zxx", "zyy", "xxyy", "xxzz", "yyzz",
]


EQUIL_SCALE = [1.0] * 10 + [1.0 / 3.0] * 6 + [1.0] * 3
SOURCE_SCALE = [1.0] * 7 + [2.0] * 3 + [1.0 / 3.0] * 6 + [1.0] * 3


def collide(f, fluid, near, coef):
    third = 1.0 / 3.0
    m = to_moments(f)
    here = near(0, 0)
    xp, xm, yp, ym = near(1, 0), near(-1, 0), near(0, 1), near(0, -1)
    dx, dy = xp - xm, yp - ym
    ring = (2.0 * here + (xp + xm)) + (yp + ym)
    pp, pm, mp, mm = near(1, 1), near(1, -1), near(-1, 1), near(-1, -1)
    a, b = pp - mm, pm - mp
    scale = (COUPLING / 36.0) * here
    fx = scale * ((2.0 * dx + (a + b)) + (roll_z(dx, 1) + roll_z(dx, -1)))
    fy = scale * ((2.0 * dy + (a - b)) + (roll_z(dy, 1) + roll_z(dy, -1)))
    fz = scale * (roll_z(ring, -1) - roll_z(ring, 1))
    rho = jnp.where(fluid, m["1"], 1.0)
    inv = 1.0 / rho
    jx, jy, jz = m["x"] + 0.5 * fx, m["y"] + 0.5 * fy, m["z"] + 0.5 * fz
    ux, uy, uz = jx * inv, jy * inv, jz * inv
    qx, qy, qz = jx * ux, jy * uy, jz * uz
    wx, wy, wz = ux * fx, uy * fy, uz * fz
    rho3 = rho * third
    base = third * (rho3 + (qx + qy + qz))
    wsum = wx + wy + wz
    wbase = (2.0 * third) * wsum
    equil = {
        "1": rho, "x": jx, "y": jy, "z": jz,
        "xy": jx * uy, "xz": jx * uz, "yz": jy * uz,
        "xx": rho3 + qx, "yy": rho3 + qy, "zz": rho3 + qz,
        "xyy": jx, "yxx": jy, "zxx": jz,
        "xxyy": base - 0.5 * qz, "xxzz": base - 0.5 * qy, "yyzz": base - 0.5 * qx,
    }
    source = {
        "1": None, "x": fx, "y": fy, "z": fz,
        "xy": fx * uy + fy * ux, "xz": fx * uz + fz * ux, "yz": fy * uz + fz * uy,
        "xx": wx, "yy": wy, "zz": wz,
        "xyy": fx, "yxx": fy, "zxx": fz,
        "xxyy": wbase - wz, "xxzz": wbase - wy, "yyzz": wbase - wx,
    }
    for table in (equil, source):
        table["xzz"], table["yzz"], table["zyy"] = table["xyy"], table["yxx"], table["zxx"]
    after = {}
    for row, name in enumerate(NAMES):
        after[name] = coef[0, row] * m[name] + coef[1, row] * equil[name]
        if source[name] is not None:
            after[name] = after[name] + coef[2, row] * source[name]
    return from_moments(after), (ux, uy, uz)


def kernel(
    counts, pop_hbm, mask_hbm, wet_hbm, wall_hbm, rate_hbm, out_hbm, vel_hbm,
    out_ref, vel_ref, pop_ref, mask_ref, wet_ref, wall_ref, rate_ref, coef,
    pot, f_buf, dens, bits, post, pot_ysend, pot_yrecv, pot_crecv,
    xa_recv, ya_send, ya_recv, xb_send, xb_recv, yb_send, yb_recv, cb_send, cb_recv,
    ox, oy, gx_d, gy_d, y_tile,
    in_sem, out_sem, pot_send_sem, pot_recv_sem, send_sem, recv_sem,
):
    nx, ny, nz = mask_ref.shape
    halves = ny // 8
    top = PAD + ny
    gx, gy = lax.axis_index("gx"), lax.axis_index("gy")
    SIGN = (-1, 1)
    leave_x, leave_y = (0, nx - 1), (0, ny - 1)
    enter_x, enter_y = (nx - 1, 0), (ny - 1, 0)
    ghost_x, ghost_y = (nx + 1, 0), (top, PAD - 1)
    XK = [ORDER[5:10], ORDER[0:5]]

    fetches = [
        pltpu.make_async_copy(a, b, in_sem.at[i])
        for i, (a, b) in enumerate(
            [
                (pop_hbm, pop_ref),
                (mask_hbm, mask_ref),
                (wet_hbm, wet_ref),
                (wall_hbm, wall_ref),
                (rate_hbm, rate_ref),
            ]
        )
    ]
    for copy in fetches:
        copy.start()

    def neighbour(d):
        return {
            "gx": lax.rem(gx + d[0] + counts[0], counts[0]),
            "gy": lax.rem(gy + d[1] + counts[1], counts[1]),
        }

    barrier = pltpu.get_barrier_semaphore()
    for d in SENDS:
        pl.semaphore_signal(
            barrier, inc=1, device_id=neighbour(d), device_id_type=pl.DeviceIdType.MESH
        )

    def remote(src, dst, sent, received, d):
        return pltpu.make_async_remote_copy(
            src_ref=src,
            dst_ref=dst,
            send_sem=sent,
            recv_sem=received,
            device_id=neighbour(d),
            device_id_type=pl.DeviceIdType.MESH,
        )

    rows = pl.ds(PAD, ny)
    xrows = pl.ds(PAD, nx)

    def pot_copies():
        pairs = {
            (1, 0): (pot.at[:, nx, rows], pot.at[:, 0, rows]),
            (-1, 0): (pot.at[:, 1, rows], pot.at[:, nx + 1, rows]),
        }
        for side, s in enumerate(SIGN):
            pairs[(0, s)] = (pot_ysend.at[side], pot_yrecv.at[side])
            for c, d in enumerate(CORNERS):
                if d[1] == s:
                    pairs[d] = (pot_ysend.at[side], pot_crecv.at[c])
        return [
            remote(*pairs[d], pot_send_sem.at[i], pot_recv_sem.at[i], d)
            for i, d in enumerate(SENDS)
        ]

    def a_copies(step, dim):
        p = step % 2
        made = []
        for m, s in enumerate(SIGN):
            if dim == "x":
                part = pl.ds(5 * (1 - m), 5)
                src = post.at[p, part, leave_x[m] + 1, rows]
                dst, i, d = xa_recv.at[step, m, :, rows], m, (s, 0)
            else:
                src = ya_send.at[step, m, :, xrows]
                dst, i, d = ya_recv.at[step, m, :, xrows], 2 + m, (0, s)
            made.append(remote(src, dst, send_sem.at[step, i], recv_sem.at[step, i], d))
        return made

    def b_copies(step, dim):
        made = []
        if dim == "corner":
            for c, d in enumerate(CORNERS):
                src, dst, i = cb_send.at[step, c], cb_recv.at[step, c], 8 + c
                made.append(remote(src, dst, send_sem.at[step, i], recv_sem.at[step, i], d))
        elif step < STEPS - 1:
            for m, s in enumerate(SIGN):
                if dim == "x":
                    src, dst, i, d = xb_send.at[step, m], xb_recv.at[step, m], 4 + m, (s, 0)
                else:
                    src, dst, i, d = yb_send.at[step, m], yb_recv.at[step, m], 6 + m, (0, s)
                made.append(remote(src, dst, send_sem.at[step, i], recv_sem.at[step, i], d))
        return made

    def clear():
        tile = jnp.zeros((8, nz), jnp.float32)
        for p in range(2):
            for m in range(2):
                for k in XK[m]:
                    for r in range((ny + 2 * PAD) // 8):
                        post[p, PLACE[k], ghost_x[m], pl.ds(8 * r, 8), :] = tile
                for k in CROSS[m]:
                    for x in range(nx):
                        post[p, PLACE[k], x + 1, pl.ds((top, 0)[m], 8), :] = tile
        for step in range(STEPS):
            for m in range(2):
                for j in range(5):
                    for r in (0, top):
                        xa_recv[step, m, j, pl.ds(r, 8), :] = tile
                    ya_send[step, m, j] = jnp.zeros((nx + 2 * PAD, nz), jnp.float32)
                    for r in (0, PAD + nx):
                        ya_recv[step, m, j, pl.ds(r, 8), :] = tile
                xb_send[step, m, pl.ds(ny, 8), :] = tile
                yb_send[step, m, 1] = jnp.zeros((nx, nz), jnp.float32)
            for c in range(4):
                cb_send[step, c] = tile

    def pot_unpack():
        for part in range(2):
            for m in range(2):
                for x in range(nx):
                    pot[part, x + 1, pl.ds(ghost_y[m], 1), :] = pot_yrecv[m, part, pl.ds(x, 1), :]
            for c, (sx, sy) in enumerate(CORNERS):
                mx, my = (sx + 1) // 2, (sy + 1) // 2
                pot[part, ghost_x[mx], pl.ds(ghost_y[my], 1), :] = pot_crecv[
                    c, part, pl.ds(leave_x[mx], 1), :
                ]

    def each_block(body, start=0, count=nx, stride=1):
        def plane(i, carry):
            for h in range(halves):
                body(start + i * stride, h)
            return carry

        lax.fori_loop(0, count, plane, 0)

    def first(x, h):
        block = pl.ds(8 * h, 8)
        fluid = mask_ref[x, block, :] == 1
        density = pop_ref[0, x, block, :]
        for k in range(1, 19):
            density = density + pop_ref[k, x, block, :]
        wet = wet_ref[x, block, :]
        wall = jnp.zeros_like(density)
        for c in range(WET_CLASSES):
            wall = wall + jnp.where(wet == c, wall_ref[c], 0.0)
        safe = jnp.where(fluid, density, 1.0)
        flag = jnp.where(fluid, 1.0, 0.0)
        for part, value in enumerate((jnp.where(fluid, 1.0 - jnp.exp(-safe), wall), flag)):
            pot[part, x + 1, pl.ds(PAD + 8 * h, 8), :] = value
            for m in range(2):
                if h == leave_y[m] // 8:
                    row = leave_y[m] % 8
                    pot_ysend[m, part, pl.ds(x, 1), :] = value[row : row + 1]

    def inflow(x, h):
        flags = jnp.zeros((8, nz), jnp.int32)
        for k, (ex, ey, ez) in enumerate(VEL):
            if k > 0:
                flag = roll_z(pot[1, x + 1 - ex, pl.ds(PAD + 8 * h - ey, 8), :], ez)
                flags = flags | jnp.where(flag == 1.0, 1 << k, 0)
        bits[x, pl.ds(8 * h, 8), :] = flags

    def collision(step, x, h):
        block = pl.ds(8 * h, 8)
        source = pop_ref if step == 0 else f_buf
        fluid = mask_ref[x, block, :] == 1
        near = lambda dx, dy: pot[0, x + 1 + dx, pl.ds(PAD + 8 * h + dy, 8), :]
        f, speed = collide([source[k, x, block, :] for k in range(19)], fluid, near, coef)
        for k in range(19):
            value = jnp.where(fluid, f[k], 0.0)
            post[step % 2, PLACE[k], x + 1, pl.ds(PAD + 8 * h, 8), :] = value
            for m in range(2):
                if k in CROSS[m] and h == leave_y[m] // 8:
                    row = leave_y[m] % 8
                    ya_send[step, m, CROSS[m].index(k), pl.ds(PAD + x, 1), :] = value[row : row + 1]
        if step == STEPS - 1:
            for c in range(3):
                vel_ref[c, x, block, :] = jnp.where(fluid, speed[c], 0.0)

    def stream(step, x, h):
        block, p = pl.ds(8 * h, 8), step % 2
        flags = bits[x, block, :]
        fluid = mask_ref[x, block, :] == 1
        density = None
        for k, (ex, ey, ez) in enumerate(VEL):
            if k == 0:
                value = post[p, PLACE[0], x + 1, pl.ds(PAD + 8 * h, 8), :]
            else:
                passed = roll_z(post[p, PLACE[k], x + 1 - ex, pl.ds(PAD + 8 * h - ey, 8), :], ez)
                bounced = post[p, PLACE[OPP[k]], x + 1, pl.ds(PAD + 8 * h, 8), :]
                value = jnp.where((flags & (1 << k)) != 0, passed, bounced)
            if step == STEPS - 1:
                out_ref[k, x, block, :] = jnp.where(fluid, value, 0.0)
            else:
                f_buf[k, x, block, :] = value
                density = value if density is None else density + value
        if step < STEPS - 1:
            dens[x, block, :] = density

    def x_sums(step):
        for m in range(2):
            for h in range(halves):
                total = None
                for k in XK[m]:
                    _, ey, ez = VEL[k]
                    value = roll_z(
                        post[step % 2, PLACE[k], leave_x[m] + 1, pl.ds(PAD + 8 * h - ey, 8), :], ez
                    )
                    total = value if total is None else total + value
                ox[m, pl.ds(8 * h, 8), :] = total

    def y_sums(step):
        for m in range(2):
            total = None
            for j, k in enumerate(CROSS[m]):
                ex, _, ez = VEL[k]
                value = roll_z(ya_send[step, m, j, pl.ds(PAD - ex, nx), :], ez)
                total = value if total is None else total + value
            oy[m] = total

    one = lambda i: pl.ds(i, 1)

    def pack_x(step):
        for m in range(2):
            xb_send[step, m, pl.ds(0, ny), :] = dens[leave_x[m]]
            for n in range(2):
                xb_send[step, m, one(ny + n), :] = oy[n, one(leave_x[m]), :]
        for c, (sx, sy) in enumerate(CORNERS):
            mx, my = (sx + 1) // 2, (sy + 1) // 2
            cb_send[step, c, 1:2, :] = dens[leave_x[mx], one(leave_y[my]), :]
            cb_send[step, c, 2:3, :] = oy[my, one(leave_x[mx]), :]
            cb_send[step, c, 3:4, :] = ox[mx, one(leave_y[my]), :]

    def pack_y(step):
        for m in range(2):
            for n in range(2):
                yb_send[step, m, 1, one(n), :] = ox[n, one(leave_y[m]), :]
            for x in range(nx):
                yb_send[step, m, 0, one(x), :] = dens[x, one(leave_y[m]), :]

    def pack_corners(step):
        for c, (sx, sy) in enumerate(CORNERS):
            mx, my = (sx + 1) // 2, (sy + 1) // 2
            j = CROSS[my].index(INDEX[(sx, sy, 0)])
            cb_send[step, c, 0:1, :] = ya_send[step, my, j, pl.ds(PAD + leave_x[mx], 1), :]

    def arrive(step, k, x, block, value):
        if step == STEPS - 1:
            fluid = mask_ref[x, block, :] == 1
            out_ref[k, x, block, :] = out_ref[k, x, block, :] + jnp.where(fluid, value, 0.0)
        else:
            f_buf[k, x, block, :] = f_buf[k, x, block, :] + value

    def x_arrive(step):
        for m in range(2):
            x = enter_x[m]
            for h in range(halves):
                block = pl.ds(8 * h, 8)
                total = None
                for j, k in enumerate(XK[m]):
                    _, ey, ez = VEL[k]
                    value = roll_z(xa_recv[step, m, j, pl.ds(PAD + 8 * h - ey, 8), :], ez)
                    arrive(step, k, x, block, value)
                    total = value if total is None else total + value
                if step < STEPS - 1:
                    dens[x, block, :] = dens[x, block, :] + total

    def y_arrive(step):
        for m in range(2):
            row = pl.ds(enter_y[m], 1)
            total = None
            for j, k in enumerate(CROSS[m]):
                ex, _, ez = VEL[k]
                value = roll_z(ya_recv[step, m, j, pl.ds(PAD - ex, nx), :], ez)
                y_tile[m, j] = value
                total = value if total is None else total + value
            y_tile[m, 5] = total
            for x in range(nx):
                for j, k in enumerate(CROSS[m]):
                    arrive(step, k, x, row, y_tile[m, j, pl.ds(x, 1), :])
                if step < STEPS - 1:
                    dens[x, row, :] = dens[x, row, :] + y_tile[m, 5, pl.ds(x, 1), :]

    def own_potential(x, h):
        block, where = pl.ds(8 * h, 8), pl.ds(PAD + 8 * h, 8)
        fluid = mask_ref[x, block, :] == 1
        value = 1.0 - jnp.exp(-dens[x, block, :])
        pot[0, x + 1, where, :] = jnp.where(fluid, value, pot[0, x + 1, where, :])

    def corners_arrive(step):
        for c, (sx, sy) in enumerate(CORNERS):
            mx, my = (sx + 1) // 2, (sy + 1) // 2
            x, y = enter_x[mx], enter_y[my]
            row = pl.ds(y, 1)
            value = cb_recv[step, c, 0:1, :]
            arrive(step, INDEX[(sx, sy, 0)], x, row, value)
            if step < STEPS - 1:
                dens[x, row, :] = dens[x, row, :] + value

    def ghost_potential(step):
        def put(x, where, density):
            flag = pot[1, x, where, :] == 1.0
            pot[0, x, where, :] = jnp.where(flag, 1.0 - jnp.exp(-density), pot[0, x, where, :])

        for m in range(2):
            gx_d[m] = xb_recv[step, m, pl.ds(0, ny), :] + ox[1 - m]
            gy_d[m] = yb_recv[step, m, 0] + oy[1 - m]
        for c, (sx, sy) in enumerate(CORNERS):
            mx, my = (sx + 1) // 2, (sy + 1) // 2
            x, y = enter_x[mx], enter_y[my]
            j = CROSS[my].index(INDEX[(-sx, sy, 0)])
            gx_d[mx, one(y), :] = gx_d[mx, one(y), :] + (
                ya_recv[step, my, j, one(PAD + x), :] + cb_recv[step, c, 2:3, :]
            )
            j = XK[mx].index(INDEX[(sx, -sy, 0)])
            gy_d[my, one(x), :] = gy_d[my, one(x), :] + (
                xa_recv[step, mx, j, one(PAD + y), :] + cb_recv[step, c, 3:4, :]
            )
            j = CROSS[1 - my].index(INDEX[(-sx, -sy, 0)])
            density = (
                cb_recv[step, c, 1:2, :] + ya_send[step, 1 - my, j, one(PAD + x), :]
            ) + (xb_recv[step, mx, one(ny + 1 - my), :] + yb_recv[step, my, 1, one(1 - mx), :])
            put(ghost_x[mx], one(ghost_y[my]), density)
        for m in range(2):
            for h in range(halves):
                put(ghost_x[m], pl.ds(PAD + 8 * h, 8), gx_d[m, pl.ds(8 * h, 8), :])
            gy_d[m] = 1.0 - jnp.exp(-gy_d[m])
            for x in range(nx):
                where = one(ghost_y[m])
                flag = pot[1, x + 1, where, :] == 1.0
                pot[0, x + 1, where, :] = jnp.where(
                    flag, gy_d[m, one(x), :], pot[0, x + 1, where, :]
                )

    for copy in fetches:
        copy.wait()
    for row in range(19):
        rate = rate_ref[row]
        coef[0, row] = 1.0 - rate
        coef[1, row] = rate * EQUIL_SCALE[row]
        coef[2, row] = (1.0 - 0.5 * rate) * SOURCE_SCALE[row]
    each_block(first)
    pl.semaphore_wait(barrier, len(SENDS))

    def start(group, swapped=()):
        if swapped:
            @pl.when(gx == counts[0] - 1)
            def _():
                for copy in swapped:
                    copy.start()

            @pl.when(gx != counts[0] - 1)
            def _():
                for copy in group:
                    copy.start()
        else:
            for copy in group:
                copy.start()
        return group

    def finish(group):
        for copy in group:
            copy.wait()

    def start_pot():
        group = pot_copies()
        order = [1, 0, 6, 7, 4, 5, 2, 3]
        return start([group[i] for i in order], [group[i] for i in (0, 1, 4, 5, 6, 7, 2, 3)])

    def start_a(step):
        group = a_copies(step, "x")
        return start(group, group[::-1])

    def start_b(step):
        group, corners = b_copies(step, "x"), b_copies(step, "corner")
        return start(group + corners[::-1], group[::-1] + corners)

    moving = start_pot()
    clear()
    finish(moving)
    pot_unpack()
    EDGE, NEXT, INNER = (0, 2, nx - 1), (1, 2, nx - 3), (2, nx - 4, 1)
    WITHIN = (1, nx - 2, 1)
    for step in range(STEPS):
        final = step == STEPS - 1
        hit = functools.partial(collision, step)
        move = functools.partial(stream, step)
        each_block(hit, *EDGE)
        x_moving = start_a(step)
        pack_corners(step)
        if not final:
            each_block(hit, *NEXT)
            if step == 0:
                each_block(inflow, *EDGE)
            each_block(move, *EDGE)
            x_sums(step)
            y_sums(step)
            pack_x(step)
        x_moving += start_b(step)
        if step == 0:
            each_block(inflow, *WITHIN)
        if final:
            each_block(hit, *NEXT)
        each_block(hit, *INNER)
        y_moving = start(a_copies(step, "y"))
        if final:
            leaving = [pltpu.make_async_copy(vel_ref, vel_hbm, out_sem.at[0])]
            leaving[0].start()
            each_block(move)
        else:
            each_block(move, *WITHIN)
            y_sums(step)
            pack_y(step)
            y_moving += start(b_copies(step, "y"))
        finish(y_moving)
        y_arrive(step)
        if final:
            for i, (x, count) in enumerate([(1, nx - 2), (0, 1), (nx - 1, 1)]):
                where = pl.ds(x, count)
                leaving.append(
                    pltpu.make_async_copy(
                        out_ref.at[:, where], out_hbm.at[:, where], out_sem.at[1 + i]
                    )
                )
            leaving[1].start()
        else:
            each_block(own_potential, *WITHIN)
        finish(x_moving)
        x_arrive(step)
        corners_arrive(step)
        if final:
            leaving[2].start()
            leaving[3].start()
            finish(leaving)
        else:
            each_block(own_potential, *EDGE)
            ghost_potential(step)


def hand_over(pop_in, vel_in, pop_out, vel_out, sem):
    copies = [pltpu.make_async_copy(vel_in, vel_out, sem.at[0])]
    for k in range(pop_in.shape[0]):
        copies.append(pltpu.make_async_copy(pop_in.at[k], pop_out.at[k], sem.at[1 + k]))
    for copy in copies:
        copy.start()
    for copy in copies:
        copy.wait()


def per_device(counts, populations, fluid_mask, wet_class, wall_potential, relax_rates):
    nx, ny, nz = fluid_mask.shape
    hbm = pl.BlockSpec(memory_space=pltpu.HBM)
    f32 = jnp.float32
    padded = (nx + 2, ny + 2 * PAD, nz)
    shapes = (
        jax.ShapeDtypeStruct((19, nx, ny, nz), f32),
        jax.ShapeDtypeStruct((3, nx, ny, nz), f32),
    )
    results = pl.pallas_call(
        functools.partial(kernel, counts),
        out_shape=shapes,
        in_specs=[hbm] * 5,
        out_specs=(hbm, hbm),
        scratch_shapes=[
            pltpu.VMEM((19, nx, ny, nz), f32),
            pltpu.VMEM((3, nx, ny, nz), f32),
            pltpu.VMEM(populations.shape, f32),
            pltpu.VMEM(fluid_mask.shape, jnp.int32),
            pltpu.VMEM(wet_class.shape, jnp.int32),
            pltpu.SMEM(wall_potential.shape, f32),
            pltpu.SMEM(relax_rates.shape, f32),
            pltpu.SMEM((3,) + relax_rates.shape, f32),
            pltpu.VMEM((2,) + padded, f32),
            pltpu.VMEM((19, nx, ny, nz), f32),
            pltpu.VMEM((nx, ny, nz), f32),
            pltpu.VMEM((nx, ny, nz), jnp.int32),
            pltpu.VMEM((2, 19) + padded, f32),
            pltpu.VMEM((2, 2, nx, nz), f32),
            pltpu.VMEM((2, 2, nx, nz), f32),
            pltpu.VMEM((4, 2, nx, nz), f32),
            pltpu.VMEM((STEPS, 2, 5, ny + 2 * PAD, nz), f32),
            pltpu.VMEM((STEPS, 2, 5, nx + 2 * PAD, nz), f32),
            pltpu.VMEM((STEPS, 2, 5, nx + 2 * PAD, nz), f32),
            pltpu.VMEM((STEPS, 2, ny + 8, nz), f32),
            pltpu.VMEM((STEPS, 2, ny + 8, nz), f32),
            pltpu.VMEM((STEPS, 2, 2, nx, nz), f32),
            pltpu.VMEM((STEPS, 2, 2, nx, nz), f32),
            pltpu.VMEM((STEPS, 4, 8, nz), f32),
            pltpu.VMEM((STEPS, 4, 8, nz), f32),
            pltpu.VMEM((2, ny, nz), f32),
            pltpu.VMEM((2, nx, nz), f32),
            pltpu.VMEM((2, ny, nz), f32),
            pltpu.VMEM((2, nx, nz), f32),
            pltpu.VMEM((2, 6, nx, nz), f32),
            pltpu.SemaphoreType.DMA((5,)),
            pltpu.SemaphoreType.DMA((4,)),
            pltpu.SemaphoreType.DMA((8,)),
            pltpu.SemaphoreType.DMA((8,)),
            pltpu.SemaphoreType.DMA((STEPS, 12)),
            pltpu.SemaphoreType.DMA((STEPS, 12)),
        ],
        compiler_params=pltpu.CompilerParams(
            collective_id=0, has_side_effects=True, vmem_limit_bytes=60 * 1024 * 1024
        ),
    )(populations, fluid_mask, wet_class, wall_potential, relax_rates)
    return pl.pallas_call(
        hand_over,
        out_shape=shapes,
        in_specs=[hbm] * 2,
        out_specs=(hbm, hbm),
        scratch_shapes=[pltpu.SemaphoreType.DMA((20,))],
        compiler_params=pltpu.CompilerParams(vmem_limit_bytes=60 * 1024 * 1024),
    )(*results)


def solution(mesh):
    counts = (mesh.shape["gx"], mesh.shape["gy"])
    return jax.shard_map(
        functools.partial(per_device, counts),
        mesh=mesh,
        in_specs=(
            P(None, ("groups", "gx"), "gy", None),
            P(("groups", "gx"), "gy", None),
            P(("groups", "gx"), "gy", None),
            P("groups"),
            P(),
        ),
        out_specs=(P(None, ("groups", "gx"), "gy", None), P(None, ("groups", "gx"), "gy", None)),
        check_vma=False,
    )
```

```python
import functools

import jax
import jax.numpy as jnp
from jax import lax
from jax.experimental import pallas as pl
from jax.experimental.pallas import tpu as pltpu
from jax.sharding import PartitionSpec as P

WET_CLASSES = 4
STEPS = 4
COUPLING = 2.5
PAD = 8
VEL = [
    (0, 0, 0),
    (1, 0, 0),
    (-1, 0, 0),
    (0, 1, 0),
    (0, -1, 0),
    (0, 0, 1),
    (0, 0, -1),
    (1, 1, 0),
    (-1, -1, 0),
    (1, -1, 0),
    (-1, 1, 0),
    (1, 0, 1),
    (-1, 0, -1),
    (1, 0, -1),
    (-1, 0, 1),
    (0, 1, 1),
    (0, -1, -1),
    (0, 1, -1),
    (0, -1, 1),
]
INDEX = {v: k for k, v in enumerate(VEL)}
OPP = [INDEX[(-a, -b, -c)] for a, b, c in VEL]
ORDER = (
    [k for k in range(19) if VEL[k][0] == 1]
    + [k for k in range(19) if VEL[k][0] == -1]
    + [k for k in range(19) if VEL[k][0] == 0]
)
PLACE = [ORDER.index(k) for k in range(19)]
CROSS = [[k for k in range(19) if VEL[k][1] == s] for s in (-1, 1)]
CORNERS = [(1, 1), (1, -1), (-1, 1), (-1, -1)]
SENDS = [(1, 0), (-1, 0), (0, 1), (0, -1)] + CORNERS


def roll_z(value, step):
    if step == 0:
        return value
    return pltpu.roll(value, step % value.shape[-1], axis=value.ndim - 1)


def to_moments(f):
    g = lambda *v: f[INDEX[v]]
    m = {}

    def plane(pp, mm, pm, mp):
        a, b, c, d = pp + mm, pm + mp, pp - mm, pm - mp
        return a + b, a - b, c + d, c - d

    m["xxyy"], m["xy"], m["xyy"], m["yxx"] = plane(
        g(1, 1, 0), g(-1, -1, 0), g(1, -1, 0), g(-1, 1, 0)
    )
    m["xxzz"], m["xz"], m["xzz"], m["zxx"] = plane(
        g(1, 0, 1), g(-1, 0, -1), g(1, 0, -1), g(-1, 0, 1)
    )
    m["yyzz"], m["yz"], m["yzz"], m["zyy"] = plane(
        g(0, 1, 1), g(0, -1, -1), g(0, 1, -1), g(0, -1, 1)
    )
    sx, dx = f[1] + f[2], f[1] - f[2]
    sy, dy = f[3] + f[4], f[3] - f[4]
    sz, dz = f[5] + f[6], f[5] - f[6]
    m["xx"] = sx + (m["xxyy"] + m["xxzz"])
    m["yy"] = sy + (m["xxyy"] + m["yyzz"])
    m["zz"] = sz + (m["xxzz"] + m["yyzz"])
    m["x"] = dx + (m["xyy"] + m["xzz"])
    m["y"] = dy + (m["yxx"] + m["yzz"])
    m["z"] = dz + (m["zxx"] + m["zyy"])
    m["1"] = ((f[0] + sx) + (sy + sz)) + ((m["xxyy"] + m["xxzz"]) + m["yyzz"])
    return m


def from_moments(m):
    f = [None] * 19

    def plane(even, cross, first, second, v):
        a, b = 0.25 * (even + cross), 0.25 * (even - cross)
        c, d = 0.25 * (first + second), 0.25 * (first - second)
        values = (a + c, a - c, b + d, b - d)
        for velocity, value in zip(v, values):
            f[INDEX[velocity]] = value

    plane(m["xxyy"], m["xy"], m["xyy"], m["yxx"], [(1, 1, 0), (-1, -1, 0), (1, -1, 0), (-1, 1, 0)])
    plane(m["xxzz"], m["xz"], m["xzz"], m["zxx"], [(1, 0, 1), (-1, 0, -1), (1, 0, -1), (-1, 0, 1)])
    plane(m["yyzz"], m["yz"], m["yzz"], m["zyy"], [(0, 1, 1), (0, -1, -1), (0, 1, -1), (0, -1, 1)])
    sx = m["xx"] - (m["xxyy"] + m["xxzz"])
    sy = m["yy"] - (m["xxyy"] + m["yyzz"])
    sz = m["zz"] - (m["xxzz"] + m["yyzz"])
    dx = m["x"] - (m["xyy"] + m["xzz"])
    dy = m["y"] - (m["yxx"] + m["yzz"])
    dz = m["z"] - (m["zxx"] + m["zyy"])
    f[1], f[2] = 0.5 * (sx + dx), 0.5 * (sx - dx)
    f[3], f[4] = 0.5 * (sy + dy), 0.5 * (sy - dy)
    f[5], f[6] = 0.5 * (sz + dz), 0.5 * (sz - dz)
    f[0] = (m["1"] - (sx + sy)) - (sz + ((m["xxyy"] + m["xxzz"]) + m["yyzz"]))
    return f


NAMES = [
    "1", "x", "y", "z", "xy", "xz", "yz", "xx", "yy", "zz",
    "xyy", "xzz", "yxx", "yzz", "zxx", "zyy", "xxyy", "xxzz", "yyzz",
]


EQUIL_SCALE = [1.0] * 10 + [1.0 / 3.0] * 6 + [1.0] * 3
SOURCE_SCALE = [1.0] * 7 + [2.0] * 3 + [1.0 / 3.0] * 6 + [1.0] * 3


def collide(f, fluid, near, coef):
    third = 1.0 / 3.0
    m = to_moments(f)
    here = near(0, 0)
    xp, xm, yp, ym = near(1, 0), near(-1, 0), near(0, 1), near(0, -1)
    dx, dy = xp - xm, yp - ym
    ring = (2.0 * here + (xp + xm)) + (yp + ym)
    pp, pm, mp, mm = near(1, 1), near(1, -1), near(-1, 1), near(-1, -1)
    a, b = pp - mm, pm - mp
    scale = (COUPLING / 36.0) * here
    fx = scale * ((2.0 * dx + (a + b)) + (roll_z(dx, 1) + roll_z(dx, -1)))
    fy = scale * ((2.0 * dy + (a - b)) + (roll_z(dy, 1) + roll_z(dy, -1)))
    fz = scale * (roll_z(ring, -1) - roll_z(ring, 1))
    rho = jnp.where(fluid, m["1"], 1.0)
    inv = 1.0 / rho
    jx, jy, jz = m["x"] + 0.5 * fx, m["y"] + 0.5 * fy, m["z"] + 0.5 * fz
    ux, uy, uz = jx * inv, jy * inv, jz * inv
    qx, qy, qz = jx * ux, jy * uy, jz * uz
    wx, wy, wz = ux * fx, uy * fy, uz * fz
    rho3 = rho * third
    base = third * (rho3 + (qx + qy + qz))
    wsum = wx + wy + wz
    wbase = (2.0 * third) * wsum
    equil = {
        "1": rho, "x": jx, "y": jy, "z": jz,
        "xy": jx * uy, "xz": jx * uz, "yz": jy * uz,
        "xx": rho3 + qx, "yy": rho3 + qy, "zz": rho3 + qz,
        "xyy": jx, "yxx": jy, "zxx": jz,
        "xxyy": base - 0.5 * qz, "xxzz": base - 0.5 * qy, "yyzz": base - 0.5 * qx,
    }
    source = {
        "1": None, "x": fx, "y": fy, "z": fz,
        "xy": fx * uy + fy * ux, "xz": fx * uz + fz * ux, "yz": fy * uz + fz * uy,
        "xx": wx, "yy": wy, "zz": wz,
        "xyy": fx, "yxx": fy, "zxx": fz,
        "xxyy": wbase - wz, "xxzz": wbase - wy, "yyzz": wbase - wx,
    }
    for table in (equil, source):
        table["xzz"], table["yzz"], table["zyy"] = table["xyy"], table["yxx"], table["zxx"]
    after = {}
    for row, name in enumerate(NAMES):
        after[name] = coef[0, row] * m[name] + coef[1, row] * equil[name]
        if source[name] is not None:
            after[name] = after[name] + coef[2, row] * source[name]
    return from_moments(after), (ux, uy, uz)


def kernel(
    counts, pop_hbm, mask_hbm, wet_hbm, wall_hbm, rate_hbm, out_hbm, vel_hbm,
    out_ref, vel_ref, pop_ref, mask_ref, wet_ref, wall_ref, rate_ref, coef,
    pot, f_buf, dens, bits, post, pot_ysend, pot_yrecv, pot_crecv,
    xa_recv, ya_send, ya_recv, xb_send, xb_recv, yb_send, yb_recv, cb_send, cb_recv,
    ox, oy, gx_d, gy_d, y_tile,
    in_sem, out_sem, pot_send_sem, pot_recv_sem, send_sem, recv_sem,
):
    nx, ny, nz = mask_ref.shape
    halves = ny // 8
    top = PAD + ny
    gx, gy = lax.axis_index("gx"), lax.axis_index("gy")
    SIGN = (-1, 1)
    leave_x, leave_y = (0, nx - 1), (0, ny - 1)
    enter_x, enter_y = (nx - 1, 0), (ny - 1, 0)
    ghost_x, ghost_y = (nx + 1, 0), (top, PAD - 1)
    XK = [ORDER[5:10], ORDER[0:5]]

    fetches = [
        pltpu.make_async_copy(a, b, in_sem.at[i])
        for i, (a, b) in enumerate(
            [
                (pop_hbm, pop_ref),
                (mask_hbm, mask_ref),
                (wet_hbm, wet_ref),
                (wall_hbm, wall_ref),
                (rate_hbm, rate_ref),
            ]
        )
    ]
    for copy in fetches:
        copy.start()

    def neighbour(d):
        return {
            "gx": lax.rem(gx + d[0] + counts[0], counts[0]),
            "gy": lax.rem(gy + d[1] + counts[1], counts[1]),
        }

    barrier = pltpu.get_barrier_semaphore()
    for d in SENDS:
        pl.semaphore_signal(
            barrier, inc=1, device_id=neighbour(d), device_id_type=pl.DeviceIdType.MESH
        )

    def remote(src, dst, sent, received, d):
        return pltpu.make_async_remote_copy(
            src_ref=src,
            dst_ref=dst,
            send_sem=sent,
            recv_sem=received,
            device_id=neighbour(d),
            device_id_type=pl.DeviceIdType.MESH,
        )

    rows = pl.ds(PAD, ny)
    xrows = pl.ds(PAD, nx)

    def pot_copies():
        pairs = {
            (1, 0): (pot.at[:, nx, rows], pot.at[:, 0, rows]),
            (-1, 0): (pot.at[:, 1, rows], pot.at[:, nx + 1, rows]),
        }
        for side, s in enumerate(SIGN):
            pairs[(0, s)] = (pot_ysend.at[side], pot_yrecv.at[side])
            for c, d in enumerate(CORNERS):
                if d[1] == s:
                    pairs[d] = (pot_ysend.at[side], pot_crecv.at[c])
        return [
            remote(*pairs[d], pot_send_sem.at[i], pot_recv_sem.at[i], d)
            for i, d in enumerate(SENDS)
        ]

    def a_copies(step, dim):
        p = step % 2
        made = []
        for m, s in enumerate(SIGN):
            if dim == "x":
                part = pl.ds(5 * (1 - m), 5)
                src = post.at[p, part, leave_x[m] + 1, rows]
                dst, i, d = xa_recv.at[step, m, :, rows], m, (s, 0)
            else:
                src = ya_send.at[step, m, :, xrows]
                dst, i, d = ya_recv.at[step, m, :, xrows], 2 + m, (0, s)
            made.append(remote(src, dst, send_sem.at[step, i], recv_sem.at[step, i], d))
        return made

    def b_copies(step, dim):
        made = []
        if dim == "corner":
            for c, d in enumerate(CORNERS):
                src, dst, i = cb_send.at[step, c], cb_recv.at[step, c], 8 + c
                made.append(remote(src, dst, send_sem.at[step, i], recv_sem.at[step, i], d))
        elif step < STEPS - 1:
            for m, s in enumerate(SIGN):
                if dim == "x":
                    src, dst, i, d = xb_send.at[step, m], xb_recv.at[step, m], 4 + m, (s, 0)
                else:
                    src, dst, i, d = yb_send.at[step, m], yb_recv.at[step, m], 6 + m, (0, s)
                made.append(remote(src, dst, send_sem.at[step, i], recv_sem.at[step, i], d))
        return made

    def clear():
        tile = jnp.zeros((8, nz), jnp.float32)
        for p in range(2):
            for m in range(2):
                for k in XK[m]:
                    for r in range((ny + 2 * PAD) // 8):
                        post[p, PLACE[k], ghost_x[m], pl.ds(8 * r, 8), :] = tile
                for k in CROSS[m]:
                    for x in range(nx):
                        post[p, PLACE[k], x + 1, pl.ds((top, 0)[m], 8), :] = tile
        for step in range(STEPS):
            for m in range(2):
                for j in range(5):
                    for r in (0, top):
                        xa_recv[step, m, j, pl.ds(r, 8), :] = tile
                    ya_send[step, m, j] = jnp.zeros((nx + 2 * PAD, nz), jnp.float32)
                    for r in (0, PAD + nx):
                        ya_recv[step, m, j, pl.ds(r, 8), :] = tile
                xb_send[step, m, pl.ds(ny, 8), :] = tile
                yb_send[step, m, 1] = jnp.zeros((nx, nz), jnp.float32)
            for c in range(4):
                cb_send[step, c] = tile

    def pot_unpack():
        for part in range(2):
            for m in range(2):
                for x in range(nx):
                    pot[part, x + 1, pl.ds(ghost_y[m], 1), :] = pot_yrecv[m, part, pl.ds(x, 1), :]
            for c, (sx, sy) in enumerate(CORNERS):
                mx, my = (sx + 1) // 2, (sy + 1) // 2
                pot[part, ghost_x[mx], pl.ds(ghost_y[my], 1), :] = pot_crecv[
                    c, part, pl.ds(leave_x[mx], 1), :
                ]

    def each_block(body, start=0, count=nx, stride=1):
        def plane(i, carry):
            for h in range(halves):
                body(start + i * stride, h)
            return carry

        lax.fori_loop(0, count, plane, 0)

    def first(x, h):
        block = pl.ds(8 * h, 8)
        fluid = mask_ref[x, block, :] == 1
        density = pop_ref[0, x, block, :]
        for k in range(1, 19):
            density = density + pop_ref[k, x, block, :]
        wet = wet_ref[x, block, :]
        wall = jnp.zeros_like(density)
        for c in range(WET_CLASSES):
            wall = wall + jnp.where(wet == c, wall_ref[c], 0.0)
        safe = jnp.where(fluid, density, 1.0)
        flag = jnp.where(fluid, 1.0, 0.0)
        for part, value in enumerate((jnp.where(fluid, 1.0 - jnp.exp(-safe), wall), flag)):
            pot[part, x + 1, pl.ds(PAD + 8 * h, 8), :] = value
            for m in range(2):
                if h == leave_y[m] // 8:
                    row = leave_y[m] % 8
                    pot_ysend[m, part, pl.ds(x, 1), :] = value[row : row + 1]

    def inflow(x, h):
        flags = jnp.zeros((8, nz), jnp.int32)
        for k, (ex, ey, ez) in enumerate(VEL):
            if k > 0:
                flag = roll_z(pot[1, x + 1 - ex, pl.ds(PAD + 8 * h - ey, 8), :], ez)
                flags = flags | jnp.where(flag == 1.0, 1 << k, 0)
        bits[x, pl.ds(8 * h, 8), :] = flags

    def collision(step, x, h):
        block = pl.ds(8 * h, 8)
        source = pop_ref if step == 0 else f_buf
        fluid = mask_ref[x, block, :] == 1
        near = lambda dx, dy: pot[0, x + 1 + dx, pl.ds(PAD + 8 * h + dy, 8), :]
        f, speed = collide([source[k, x, block, :] for k in range(19)], fluid, near, coef)
        for k in range(19):
            value = jnp.where(fluid, f[k], 0.0)
            post[step % 2, PLACE[k], x + 1, pl.ds(PAD + 8 * h, 8), :] = value
            for m in range(2):
                if k in CROSS[m] and h == leave_y[m] // 8:
                    row = leave_y[m] % 8
                    ya_send[step, m, CROSS[m].index(k), pl.ds(PAD + x, 1), :] = value[row : row + 1]
        if step == STEPS - 1:
            for c in range(3):
                vel_ref[c, x, block, :] = jnp.where(fluid, speed[c], 0.0)

    def stream(step, x, h):
        block, p = pl.ds(8 * h, 8), step % 2
        flags = bits[x, block, :]
        fluid = mask_ref[x, block, :] == 1
        density = None
        for k, (ex, ey, ez) in enumerate(VEL):
            if k == 0:
                value = post[p, PLACE[0], x + 1, pl.ds(PAD + 8 * h, 8), :]
            else:
                passed = roll_z(post[p, PLACE[k], x + 1 - ex, pl.ds(PAD + 8 * h - ey, 8), :], ez)
                bounced = post[p, PLACE[OPP[k]], x + 1, pl.ds(PAD + 8 * h, 8), :]
                value = jnp.where((flags & (1 << k)) != 0, passed, bounced)
            if step == STEPS - 1:
                out_ref[k, x, block, :] = jnp.where(fluid, value, 0.0)
            else:
                f_buf[k, x, block, :] = value
                density = value if density is None else density + value
        if step < STEPS - 1:
            dens[x, block, :] = density

    def x_sums(step):
        for m in range(2):
            for h in range(halves):
                total = None
                for k in XK[m]:
                    _, ey, ez = VEL[k]
                    value = roll_z(
                        post[step % 2, PLACE[k], leave_x[m] + 1, pl.ds(PAD + 8 * h - ey, 8), :], ez
                    )
                    total = value if total is None else total + value
                ox[m, pl.ds(8 * h, 8), :] = total

    def y_sums(step):
        for m in range(2):
            total = None
            for j, k in enumerate(CROSS[m]):
                ex, _, ez = VEL[k]
                value = roll_z(ya_send[step, m, j, pl.ds(PAD - ex, nx), :], ez)
                total = value if total is None else total + value
            oy[m] = total

    one = lambda i: pl.ds(i, 1)

    def pack_x(step):
        for m in range(2):
            xb_send[step, m, pl.ds(0, ny), :] = dens[leave_x[m]]
            for n in range(2):
                xb_send[step, m, one(ny + n), :] = oy[n, one(leave_x[m]), :]
        for c, (sx, sy) in enumerate(CORNERS):
            mx, my = (sx + 1) // 2, (sy + 1) // 2
            cb_send[step, c, 1:2, :] = dens[leave_x[mx], one(leave_y[my]), :]
            cb_send[step, c, 2:3, :] = oy[my, one(leave_x[mx]), :]
            cb_send[step, c, 3:4, :] = ox[mx, one(leave_y[my]), :]

    def pack_y(step):
        for m in range(2):
            for n in range(2):
                yb_send[step, m, 1, one(n), :] = ox[n, one(leave_y[m]), :]
            for x in range(nx):
                yb_send[step, m, 0, one(x), :] = dens[x, one(leave_y[m]), :]

    def pack_corners(step):
        for c, (sx, sy) in enumerate(CORNERS):
            mx, my = (sx + 1) // 2, (sy + 1) // 2
            j = CROSS[my].index(INDEX[(sx, sy, 0)])
            cb_send[step, c, 0:1, :] = ya_send[step, my, j, pl.ds(PAD + leave_x[mx], 1), :]

    def arrive(step, k, x, block, value):
        if step == STEPS - 1:
            fluid = mask_ref[x, block, :] == 1
            out_ref[k, x, block, :] = out_ref[k, x, block, :] + jnp.where(fluid, value, 0.0)
        else:
            f_buf[k, x, block, :] = f_buf[k, x, block, :] + value

    def x_arrive(step):
        for m in range(2):
            x = enter_x[m]
            for h in range(halves):
                block = pl.ds(8 * h, 8)
                total = None
                for j, k in enumerate(XK[m]):
                    _, ey, ez = VEL[k]
                    value = roll_z(xa_recv[step, m, j, pl.ds(PAD + 8 * h - ey, 8), :], ez)
                    arrive(step, k, x, block, value)
                    total = value if total is None else total + value
                if step < STEPS - 1:
                    dens[x, block, :] = dens[x, block, :] + total

    def y_arrive(step):
        for m in range(2):
            row = pl.ds(enter_y[m], 1)
            total = None
            for j, k in enumerate(CROSS[m]):
                ex, _, ez = VEL[k]
                value = roll_z(ya_recv[step, m, j, pl.ds(PAD - ex, nx), :], ez)
                y_tile[m, j] = value
                total = value if total is None else total + value
            y_tile[m, 5] = total
            for x in range(nx):
                for j, k in enumerate(CROSS[m]):
                    arrive(step, k, x, row, y_tile[m, j, pl.ds(x, 1), :])
                if step < STEPS - 1:
                    dens[x, row, :] = dens[x, row, :] + y_tile[m, 5, pl.ds(x, 1), :]

    def own_potential(x, h):
        block, where = pl.ds(8 * h, 8), pl.ds(PAD + 8 * h, 8)
        fluid = mask_ref[x, block, :] == 1
        value = 1.0 - jnp.exp(-dens[x, block, :])
        pot[0, x + 1, where, :] = jnp.where(fluid, value, pot[0, x + 1, where, :])

    def corners_arrive(step):
        for c, (sx, sy) in enumerate(CORNERS):
            mx, my = (sx + 1) // 2, (sy + 1) // 2
            x, y = enter_x[mx], enter_y[my]
            row = pl.ds(y, 1)
            value = cb_recv[step, c, 0:1, :]
            arrive(step, INDEX[(sx, sy, 0)], x, row, value)
            if step < STEPS - 1:
                dens[x, row, :] = dens[x, row, :] + value

    def ghost_potential(step):
        def put(x, where, density):
            flag = pot[1, x, where, :] == 1.0
            pot[0, x, where, :] = jnp.where(flag, 1.0 - jnp.exp(-density), pot[0, x, where, :])

        for m in range(2):
            gx_d[m] = xb_recv[step, m, pl.ds(0, ny), :] + ox[1 - m]
            gy_d[m] = yb_recv[step, m, 0] + oy[1 - m]
        for c, (sx, sy) in enumerate(CORNERS):
            mx, my = (sx + 1) // 2, (sy + 1) // 2
            x, y = enter_x[mx], enter_y[my]
            j = CROSS[my].index(INDEX[(-sx, sy, 0)])
            gx_d[mx, one(y), :] = gx_d[mx, one(y), :] + (
                ya_recv[step, my, j, one(PAD + x), :] + cb_recv[step, c, 2:3, :]
            )
            j = XK[mx].index(INDEX[(sx, -sy, 0)])
            gy_d[my, one(x), :] = gy_d[my, one(x), :] + (
                xa_recv[step, mx, j, one(PAD + y), :] + cb_recv[step, c, 3:4, :]
            )
            j = CROSS[1 - my].index(INDEX[(-sx, -sy, 0)])
            density = (
                cb_recv[step, c, 1:2, :] + ya_send[step, 1 - my, j, one(PAD + x), :]
            ) + (xb_recv[step, mx, one(ny + 1 - my), :] + yb_recv[step, my, 1, one(1 - mx), :])
            put(ghost_x[mx], one(ghost_y[my]), density)
        for m in range(2):
            for h in range(halves):
                put(ghost_x[m], pl.ds(PAD + 8 * h, 8), gx_d[m, pl.ds(8 * h, 8), :])
            gy_d[m] = 1.0 - jnp.exp(-gy_d[m])
            for x in range(nx):
                where = one(ghost_y[m])
                flag = pot[1, x + 1, where, :] == 1.0
                pot[0, x + 1, where, :] = jnp.where(
                    flag, gy_d[m, one(x), :], pot[0, x + 1, where, :]
                )

    for copy in fetches:
        copy.wait()
    for row in range(19):
        rate = rate_ref[row]
        coef[0, row] = 1.0 - rate
        coef[1, row] = rate * EQUIL_SCALE[row]
        coef[2, row] = (1.0 - 0.5 * rate) * SOURCE_SCALE[row]
    each_block(first)
    pl.semaphore_wait(barrier, len(SENDS))

    def start(group, swapped=()):
        if swapped:
            @pl.when(gx == counts[0] - 1)
            def _():
                for copy in swapped:
                    copy.start()

            @pl.when(gx != counts[0] - 1)
            def _():
                for copy in group:
                    copy.start()
        else:
            for copy in group:
                copy.start()
        return group

    def finish(group):
        for copy in group:
            copy.wait()

    def start_pot():
        group = pot_copies()
        order = [1, 0, 6, 7, 4, 5, 2, 3]
        return start([group[i] for i in order], [group[i] for i in (0, 1, 4, 5, 6, 7, 2, 3)])

    def start_a(step):
        group = a_copies(step, "x")
        return start(group, group[::-1])

    def start_b(step):
        group, corners = b_copies(step, "x"), b_copies(step, "corner")
        return start(group + corners[::-1], group[::-1] + corners)

    moving = start_pot()
    clear()
    finish(moving)
    pot_unpack()
    EDGE, NEXT, INNER = (0, 2, nx - 1), (1, 2, nx - 3), (2, nx - 4, 1)
    WITHIN = (1, nx - 2, 1)
    for step in range(STEPS):
        final = step == STEPS - 1
        hit = functools.partial(collision, step)
        move = functools.partial(stream, step)
        each_block(hit, *EDGE)
        x_moving = start_a(step)
        pack_corners(step)
        if not final:
            each_block(hit, *NEXT)
            if step == 0:
                each_block(inflow, *EDGE)
            each_block(move, *EDGE)
            x_sums(step)
            y_sums(step)
            pack_x(step)
        b_moving = start_b(step)
        if step == 0:
            each_block(inflow, *WITHIN)
        if final:
            each_block(hit, *NEXT)
        each_block(hit, *INNER)
        y_moving = start(a_copies(step, "y"))
        if final:
            leaving = [pltpu.make_async_copy(vel_ref, vel_hbm, out_sem.at[0])]
            leaving[0].start()
            each_block(move)
        else:
            each_block(move, *WITHIN)
            y_sums(step)
            pack_y(step)
            b_moving += start(b_copies(step, "y"))
        finish(y_moving)
        y_arrive(step)
        if final:
            for i, (x, count) in enumerate([(1, nx - 2), (0, 1), (nx - 1, 1)]):
                where = pl.ds(x, count)
                leaving.append(
                    pltpu.make_async_copy(
                        out_ref.at[:, where], out_hbm.at[:, where], out_sem.at[1 + i]
                    )
                )
            leaving[1].start()
        else:
            each_block(own_potential, *WITHIN)
        finish(x_moving)
        x_arrive(step)
        finish(b_moving)
        corners_arrive(step)
        if final:
            leaving[2].start()
            leaving[3].start()
            finish(leaving)
        else:
            each_block(own_potential, *EDGE)
            ghost_potential(step)


CHUNK = 5


def hand_over(pop_in, vel_in, pop_out, vel_out, pop, vel, in_sem, out_sem):
    parts = [(pop_in, pop, pop_out, k) for k in range(0, pop_in.shape[0], CHUNK)]
    parts.append((vel_in, vel, vel_out, 0))
    inward, outward = [], []
    for i, (src, held, dst, k) in enumerate(parts):
        where = pl.ds(k, min(CHUNK, src.shape[0] - k))
        inward.append(pltpu.make_async_copy(src.at[where], held.at[where], in_sem.at[i]))
        outward.append(pltpu.make_async_copy(held.at[where], dst.at[where], out_sem.at[i]))
    for copy in inward:
        copy.start()
    for arriving, leaving in zip(inward, outward):
        arriving.wait()
        leaving.start()
    for copy in outward:
        copy.wait()


def per_device(counts, populations, fluid_mask, wet_class, wall_potential, relax_rates):
    nx, ny, nz = fluid_mask.shape
    hbm = pl.BlockSpec(memory_space=pltpu.HBM)
    f32 = jnp.float32
    padded = (nx + 2, ny + 2 * PAD, nz)
    shapes = (
        jax.ShapeDtypeStruct((19, nx, ny, nz), f32),
        jax.ShapeDtypeStruct((3, nx, ny, nz), f32),
    )
    results = pl.pallas_call(
        functools.partial(kernel, counts),
        out_shape=shapes,
        in_specs=[hbm] * 5,
        out_specs=(hbm, hbm),
        scratch_shapes=[
            pltpu.VMEM((19, nx, ny, nz), f32),
            pltpu.VMEM((3, nx, ny, nz), f32),
            pltpu.VMEM(populations.shape, f32),
            pltpu.VMEM(fluid_mask.shape, jnp.int32),
            pltpu.VMEM(wet_class.shape, jnp.int32),
            pltpu.SMEM(wall_potential.shape, f32),
            pltpu.SMEM(relax_rates.shape, f32),
            pltpu.SMEM((3,) + relax_rates.shape, f32),
            pltpu.VMEM((2,) + padded, f32),
            pltpu.VMEM((19, nx, ny, nz), f32),
            pltpu.VMEM((nx, ny, nz), f32),
            pltpu.VMEM((nx, ny, nz), jnp.int32),
            pltpu.VMEM((2, 19) + padded, f32),
            pltpu.VMEM((2, 2, nx, nz), f32),
            pltpu.VMEM((2, 2, nx, nz), f32),
            pltpu.VMEM((4, 2, nx, nz), f32),
            pltpu.VMEM((STEPS, 2, 5, ny + 2 * PAD, nz), f32),
            pltpu.VMEM((STEPS, 2, 5, nx + 2 * PAD, nz), f32),
            pltpu.VMEM((STEPS, 2, 5, nx + 2 * PAD, nz), f32),
            pltpu.VMEM((STEPS, 2, ny + 8, nz), f32),
            pltpu.VMEM((STEPS, 2, ny + 8, nz), f32),
            pltpu.VMEM((STEPS, 2, 2, nx, nz), f32),
            pltpu.VMEM((STEPS, 2, 2, nx, nz), f32),
            pltpu.VMEM((STEPS, 4, 8, nz), f32),
            pltpu.VMEM((STEPS, 4, 8, nz), f32),
            pltpu.VMEM((2, ny, nz), f32),
            pltpu.VMEM((2, nx, nz), f32),
            pltpu.VMEM((2, ny, nz), f32),
            pltpu.VMEM((2, nx, nz), f32),
            pltpu.VMEM((2, 6, nx, nz), f32),
            pltpu.SemaphoreType.DMA((5,)),
            pltpu.SemaphoreType.DMA((4,)),
            pltpu.SemaphoreType.DMA((8,)),
            pltpu.SemaphoreType.DMA((8,)),
            pltpu.SemaphoreType.DMA((STEPS, 12)),
            pltpu.SemaphoreType.DMA((STEPS, 12)),
        ],
        compiler_params=pltpu.CompilerParams(
            collective_id=0, has_side_effects=True, vmem_limit_bytes=60 * 1024 * 1024
        ),
    )(populations, fluid_mask, wet_class, wall_potential, relax_rates)
    return pl.pallas_call(
        hand_over,
        out_shape=shapes,
        in_specs=[hbm] * 2,
        out_specs=(hbm, hbm),
        scratch_shapes=[pltpu.VMEM(shape.shape, f32) for shape in shapes]
        + [pltpu.SemaphoreType.DMA((-(-19 // CHUNK) + 1,))] * 2,
        compiler_params=pltpu.CompilerParams(vmem_limit_bytes=60 * 1024 * 1024),
    )(*results)


def solution(mesh):
    counts = (mesh.shape["gx"], mesh.shape["gy"])
    return jax.shard_map(
        functools.partial(per_device, counts),
        mesh=mesh,
        in_specs=(
            P(None, ("groups", "gx"), "gy", None),
            P(("groups", "gx"), "gy", None),
            P(("groups", "gx"), "gy", None),
            P("groups"),
            P(),
        ),
        out_specs=(P(None, ("groups", "gx"), "gy", None), P(None, ("groups", "gx"), "gy", None)),
        check_vma=False,
    )
```

```python
import functools

import jax
import jax.numpy as jnp
from jax import lax
from jax.experimental import pallas as pl
from jax.experimental.pallas import tpu as pltpu
from jax.sharding import PartitionSpec as P

WET_CLASSES = 4
STEPS = 4
COUPLING = 2.5
PAD = 8
VEL = [
    (0, 0, 0),
    (1, 0, 0),
    (-1, 0, 0),
    (0, 1, 0),
    (0, -1, 0),
    (0, 0, 1),
    (0, 0, -1),
    (1, 1, 0),
    (-1, -1, 0),
    (1, -1, 0),
    (-1, 1, 0),
    (1, 0, 1),
    (-1, 0, -1),
    (1, 0, -1),
    (-1, 0, 1),
    (0, 1, 1),
    (0, -1, -1),
    (0, 1, -1),
    (0, -1, 1),
]
INDEX = {v: k for k, v in enumerate(VEL)}
OPP = [INDEX[(-a, -b, -c)] for a, b, c in VEL]
ORDER = (
    [k for k in range(19) if VEL[k][0] == 1]
    + [k for k in range(19) if VEL[k][0] == -1]
    + [k for k in range(19) if VEL[k][0] == 0]
)
PLACE = [ORDER.index(k) for k in range(19)]
CROSS = [[k for k in range(19) if VEL[k][1] == s] for s in (-1, 1)]
CORNERS = [(1, 1), (1, -1), (-1, 1), (-1, -1)]
SENDS = [(1, 0), (-1, 0), (0, 1), (0, -1)] + CORNERS


def roll_z(value, step):
    if step == 0:
        return value
    return pltpu.roll(value, step % value.shape[-1], axis=value.ndim - 1)


def to_moments(f):
    g = lambda *v: f[INDEX[v]]
    m = {}

    def plane(pp, mm, pm, mp):
        a, b, c, d = pp + mm, pm + mp, pp - mm, pm - mp
        return a + b, a - b, c + d, c - d

    m["xxyy"], m["xy"], m["xyy"], m["yxx"] = plane(
        g(1, 1, 0), g(-1, -1, 0), g(1, -1, 0), g(-1, 1, 0)
    )
    m["xxzz"], m["xz"], m["xzz"], m["zxx"] = plane(
        g(1, 0, 1), g(-1, 0, -1), g(1, 0, -1), g(-1, 0, 1)
    )
    m["yyzz"], m["yz"], m["yzz"], m["zyy"] = plane(
        g(0, 1, 1), g(0, -1, -1), g(0, 1, -1), g(0, -1, 1)
    )
    sx, dx = f[1] + f[2], f[1] - f[2]
    sy, dy = f[3] + f[4], f[3] - f[4]
    sz, dz = f[5] + f[6], f[5] - f[6]
    m["xx"] = sx + (m["xxyy"] + m["xxzz"])
    m["yy"] = sy + (m["xxyy"] + m["yyzz"])
    m["zz"] = sz + (m["xxzz"] + m["yyzz"])
    m["x"] = dx + (m["xyy"] + m["xzz"])
    m["y"] = dy + (m["yxx"] + m["yzz"])
    m["z"] = dz + (m["zxx"] + m["zyy"])
    m["1"] = ((f[0] + sx) + (sy + sz)) + ((m["xxyy"] + m["xxzz"]) + m["yyzz"])
    return m


def from_moments(m):
    f = [None] * 19

    def plane(even, cross, first, second, v):
        a, b = 0.25 * (even + cross), 0.25 * (even - cross)
        c, d = 0.25 * (first + second), 0.25 * (first - second)
        values = (a + c, a - c, b + d, b - d)
        for velocity, value in zip(v, values):
            f[INDEX[velocity]] = value

    plane(m["xxyy"], m["xy"], m["xyy"], m["yxx"], [(1, 1, 0), (-1, -1, 0), (1, -1, 0), (-1, 1, 0)])
    plane(m["xxzz"], m["xz"], m["xzz"], m["zxx"], [(1, 0, 1), (-1, 0, -1), (1, 0, -1), (-1, 0, 1)])
    plane(m["yyzz"], m["yz"], m["yzz"], m["zyy"], [(0, 1, 1), (0, -1, -1), (0, 1, -1), (0, -1, 1)])
    sx = m["xx"] - (m["xxyy"] + m["xxzz"])
    sy = m["yy"] - (m["xxyy"] + m["yyzz"])
    sz = m["zz"] - (m["xxzz"] + m["yyzz"])
    dx = m["x"] - (m["xyy"] + m["xzz"])
    dy = m["y"] - (m["yxx"] + m["yzz"])
    dz = m["z"] - (m["zxx"] + m["zyy"])
    f[1], f[2] = 0.5 * (sx + dx), 0.5 * (sx - dx)
    f[3], f[4] = 0.5 * (sy + dy), 0.5 * (sy - dy)
    f[5], f[6] = 0.5 * (sz + dz), 0.5 * (sz - dz)
    f[0] = (m["1"] - (sx + sy)) - (sz + ((m["xxyy"] + m["xxzz"]) + m["yyzz"]))
    return f


NAMES = [
    "1", "x", "y", "z", "xy", "xz", "yz", "xx", "yy", "zz",
    "xyy", "xzz", "yxx", "yzz", "zxx", "zyy", "xxyy", "xxzz", "yyzz",
]


EQUIL_SCALE = [1.0] * 10 + [1.0 / 3.0] * 6 + [1.0] * 3
SOURCE_SCALE = [1.0] * 7 + [2.0] * 3 + [1.0 / 3.0] * 6 + [1.0] * 3


def collide(f, fluid, near, coef):
    third = 1.0 / 3.0
    m = to_moments(f)
    here = near(0, 0)
    xp, xm, yp, ym = near(1, 0), near(-1, 0), near(0, 1), near(0, -1)
    dx, dy = xp - xm, yp - ym
    ring = (2.0 * here + (xp + xm)) + (yp + ym)
    pp, pm, mp, mm = near(1, 1), near(1, -1), near(-1, 1), near(-1, -1)
    a, b = pp - mm, pm - mp
    scale = (COUPLING / 36.0) * here
    fx = scale * ((2.0 * dx + (a + b)) + (roll_z(dx, 1) + roll_z(dx, -1)))
    fy = scale * ((2.0 * dy + (a - b)) + (roll_z(dy, 1) + roll_z(dy, -1)))
    fz = scale * (roll_z(ring, -1) - roll_z(ring, 1))
    rho = jnp.where(fluid, m["1"], 1.0)
    inv = 1.0 / rho
    jx, jy, jz = m["x"] + 0.5 * fx, m["y"] + 0.5 * fy, m["z"] + 0.5 * fz
    ux, uy, uz = jx * inv, jy * inv, jz * inv
    qx, qy, qz = jx * ux, jy * uy, jz * uz
    wx, wy, wz = ux * fx, uy * fy, uz * fz
    rho3 = rho * third
    base = third * (rho3 + (qx + qy + qz))
    wsum = wx + wy + wz
    wbase = (2.0 * third) * wsum
    equil = {
        "1": rho, "x": jx, "y": jy, "z": jz,
        "xy": jx * uy, "xz": jx * uz, "yz": jy * uz,
        "xx": rho3 + qx, "yy": rho3 + qy, "zz": rho3 + qz,
        "xyy": jx, "yxx": jy, "zxx": jz,
        "xxyy": base - 0.5 * qz, "xxzz": base - 0.5 * qy, "yyzz": base - 0.5 * qx,
    }
    source = {
        "1": None, "x": fx, "y": fy, "z": fz,
        "xy": fx * uy + fy * ux, "xz": fx * uz + fz * ux, "yz": fy * uz + fz * uy,
        "xx": wx, "yy": wy, "zz": wz,
        "xyy": fx, "yxx": fy, "zxx": fz,
        "xxyy": wbase - wz, "xxzz": wbase - wy, "yyzz": wbase - wx,
    }
    for table in (equil, source):
        table["xzz"], table["yzz"], table["zyy"] = table["xyy"], table["yxx"], table["zxx"]
    after = {}
    for row, name in enumerate(NAMES):
        after[name] = coef[0, row] * m[name] + coef[1, row] * equil[name]
        if source[name] is not None:
            after[name] = after[name] + coef[2, row] * source[name]
    return from_moments(after), (ux, uy, uz)


def kernel(
    counts, pop_hbm, mask_hbm, wet_hbm, wall_hbm, rate_hbm, out_hbm, vel_hbm,
    out_ref, vel_ref, pop_ref, mask_ref, wet_ref, wall_ref, rate_ref, coef,
    pot, f_buf, dens, bits, post, pot_ysend, pot_yrecv, pot_crecv,
    xa_recv, ya_send, ya_recv, xb_send, xb_recv, yb_send, yb_recv, cb_send, cb_recv,
    ox, oy, gx_d, gy_d, y_tile,
    in_sem, out_sem, pot_send_sem, pot_recv_sem, send_sem, recv_sem,
):
    nx, ny, nz = mask_ref.shape
    halves = ny // 8
    top = PAD + ny
    gx, gy = lax.axis_index("gx"), lax.axis_index("gy")
    SIGN = (-1, 1)
    leave_x, leave_y = (0, nx - 1), (0, ny - 1)
    enter_x, enter_y = (nx - 1, 0), (ny - 1, 0)
    ghost_x, ghost_y = (nx + 1, 0), (top, PAD - 1)
    XK = [ORDER[5:10], ORDER[0:5]]

    fetches = [
        pltpu.make_async_copy(a, b, in_sem.at[i])
        for i, (a, b) in enumerate(
            [
                (pop_hbm, pop_ref),
                (mask_hbm, mask_ref),
                (wet_hbm, wet_ref),
                (wall_hbm, wall_ref),
                (rate_hbm, rate_ref),
            ]
        )
    ]
    for copy in fetches:
        copy.start()

    def neighbour(d):
        return {
            "gx": lax.rem(gx + d[0] + counts[0], counts[0]),
            "gy": lax.rem(gy + d[1] + counts[1], counts[1]),
        }

    barrier = pltpu.get_barrier_semaphore()
    for d in SENDS:
        pl.semaphore_signal(
            barrier, inc=1, device_id=neighbour(d), device_id_type=pl.DeviceIdType.MESH
        )

    def remote(src, dst, sent, received, d):
        return pltpu.make_async_remote_copy(
            src_ref=src,
            dst_ref=dst,
            send_sem=sent,
            recv_sem=received,
            device_id=neighbour(d),
            device_id_type=pl.DeviceIdType.MESH,
        )

    rows = pl.ds(PAD, ny)
    xrows = pl.ds(PAD, nx)

    def pot_copies():
        pairs = {
            (1, 0): (pot.at[:, nx, rows], pot.at[:, 0, rows]),
            (-1, 0): (pot.at[:, 1, rows], pot.at[:, nx + 1, rows]),
        }
        for side, s in enumerate(SIGN):
            pairs[(0, s)] = (pot_ysend.at[side], pot_yrecv.at[side])
            for c, d in enumerate(CORNERS):
                if d[1] == s:
                    pairs[d] = (pot_ysend.at[side], pot_crecv.at[c])
        return [
            remote(*pairs[d], pot_send_sem.at[i], pot_recv_sem.at[i], d)
            for i, d in enumerate(SENDS)
        ]

    def a_copies(step, dim):
        p = step % 2
        made = []
        for m, s in enumerate(SIGN):
            if dim == "x":
                part = pl.ds(5 * (1 - m), 5)
                src = post.at[p, part, leave_x[m] + 1, rows]
                dst, i, d = xa_recv.at[step, m, :, rows], m, (s, 0)
            else:
                src = ya_send.at[step, m, :, xrows]
                dst, i, d = ya_recv.at[step, m, :, xrows], 2 + m, (0, s)
            made.append(remote(src, dst, send_sem.at[step, i], recv_sem.at[step, i], d))
        return made

    def b_copies(step, dim):
        made = []
        if dim == "corner":
            for c, d in enumerate(CORNERS):
                src, dst, i = cb_send.at[step, c], cb_recv.at[step, c], 8 + c
                made.append(remote(src, dst, send_sem.at[step, i], recv_sem.at[step, i], d))
        elif step < STEPS - 1:
            for m, s in enumerate(SIGN):
                if dim == "x":
                    src, dst, i, d = xb_send.at[step, m], xb_recv.at[step, m], 4 + m, (s, 0)
                else:
                    src, dst, i, d = yb_send.at[step, m], yb_recv.at[step, m], 6 + m, (0, s)
                made.append(remote(src, dst, send_sem.at[step, i], recv_sem.at[step, i], d))
        return made

    def clear():
        tile = jnp.zeros((8, nz), jnp.float32)
        for p in range(2):
            for m in range(2):
                for k in XK[m]:
                    for r in range((ny + 2 * PAD) // 8):
                        post[p, PLACE[k], ghost_x[m], pl.ds(8 * r, 8), :] = tile
                for k in CROSS[m]:
                    for x in range(nx):
                        post[p, PLACE[k], x + 1, pl.ds((top, 0)[m], 8), :] = tile
        for step in range(STEPS):
            for m in range(2):
                for j in range(5):
                    for r in (0, top):
                        xa_recv[step, m, j, pl.ds(r, 8), :] = tile
                    ya_send[step, m, j] = jnp.zeros((nx + 2 * PAD, nz), jnp.float32)
                    for r in (0, PAD + nx):
                        ya_recv[step, m, j, pl.ds(r, 8), :] = tile
                xb_send[step, m, pl.ds(ny, 8), :] = tile
                yb_send[step, m, 1] = jnp.zeros((nx, nz), jnp.float32)
            for c in range(4):
                cb_send[step, c] = tile

    def pot_unpack():
        for part in range(2):
            for m in range(2):
                for x in range(nx):
                    pot[part, x + 1, pl.ds(ghost_y[m], 1), :] = pot_yrecv[m, part, pl.ds(x, 1), :]
            for c, (sx, sy) in enumerate(CORNERS):
                mx, my = (sx + 1) // 2, (sy + 1) // 2
                pot[part, ghost_x[mx], pl.ds(ghost_y[my], 1), :] = pot_crecv[
                    c, part, pl.ds(leave_x[mx], 1), :
                ]

    def each_block(body, start=0, count=nx, stride=1, group=1):
        group = group if count % group == 0 else 1

        def planes(i, carry):
            for j in range(group):
                for h in range(halves):
                    body(start + (i * group + j) * stride, h)
            return carry

        if count == group:
            planes(0, 0)
        else:
            lax.fori_loop(0, count // group, planes, 0)

    def first(x, h):
        block = pl.ds(8 * h, 8)
        fluid = mask_ref[x, block, :] == 1
        density = pop_ref[0, x, block, :]
        for k in range(1, 19):
            density = density + pop_ref[k, x, block, :]
        wet = wet_ref[x, block, :]
        wall = jnp.zeros_like(density)
        for c in range(WET_CLASSES):
            wall = wall + jnp.where(wet == c, wall_ref[c], 0.0)
        safe = jnp.where(fluid, density, 1.0)
        flag = jnp.where(fluid, 1.0, 0.0)
        for part, value in enumerate((jnp.where(fluid, 1.0 - jnp.exp(-safe), wall), flag)):
            pot[part, x + 1, pl.ds(PAD + 8 * h, 8), :] = value
            for m in range(2):
                if h == leave_y[m] // 8:
                    row = leave_y[m] % 8
                    pot_ysend[m, part, pl.ds(x, 1), :] = value[row : row + 1]

    def inflow(x, h):
        flags = jnp.zeros((8, nz), jnp.int32)
        for k, (ex, ey, ez) in enumerate(VEL):
            if k > 0:
                flag = roll_z(pot[1, x + 1 - ex, pl.ds(PAD + 8 * h - ey, 8), :], ez)
                flags = flags | jnp.where(flag == 1.0, 1 << k, 0)
        bits[x, pl.ds(8 * h, 8), :] = flags

    def collision(step, x, h):
        block = pl.ds(8 * h, 8)
        source = pop_ref if step == 0 else f_buf
        fluid = mask_ref[x, block, :] == 1
        near = lambda dx, dy: pot[0, x + 1 + dx, pl.ds(PAD + 8 * h + dy, 8), :]
        f, speed = collide([source[k, x, block, :] for k in range(19)], fluid, near, coef)
        for k in range(19):
            value = jnp.where(fluid, f[k], 0.0)
            post[step % 2, PLACE[k], x + 1, pl.ds(PAD + 8 * h, 8), :] = value
            for m in range(2):
                if k in CROSS[m] and h == leave_y[m] // 8:
                    row = leave_y[m] % 8
                    ya_send[step, m, CROSS[m].index(k), pl.ds(PAD + x, 1), :] = value[row : row + 1]
        if step == STEPS - 1:
            for c in range(3):
                vel_ref[c, x, block, :] = jnp.where(fluid, speed[c], 0.0)

    def stream(step, x, h):
        block, p = pl.ds(8 * h, 8), step % 2
        flags = bits[x, block, :]
        fluid = mask_ref[x, block, :] == 1
        density = None
        for k, (ex, ey, ez) in enumerate(VEL):
            if k == 0:
                value = post[p, PLACE[0], x + 1, pl.ds(PAD + 8 * h, 8), :]
            else:
                passed = roll_z(post[p, PLACE[k], x + 1 - ex, pl.ds(PAD + 8 * h - ey, 8), :], ez)
                bounced = post[p, PLACE[OPP[k]], x + 1, pl.ds(PAD + 8 * h, 8), :]
                value = jnp.where((flags & (1 << k)) != 0, passed, bounced)
            if step == STEPS - 1:
                out_ref[k, x, block, :] = jnp.where(fluid, value, 0.0)
            else:
                f_buf[k, x, block, :] = value
                density = value if density is None else density + value
        if step < STEPS - 1:
            dens[x, block, :] = density

    def x_sums(step):
        for m in range(2):
            for h in range(halves):
                total = None
                for k in XK[m]:
                    _, ey, ez = VEL[k]
                    value = roll_z(
                        post[step % 2, PLACE[k], leave_x[m] + 1, pl.ds(PAD + 8 * h - ey, 8), :], ez
                    )
                    total = value if total is None else total + value
                ox[m, pl.ds(8 * h, 8), :] = total

    def y_sums(step):
        for m in range(2):
            total = None
            for j, k in enumerate(CROSS[m]):
                ex, _, ez = VEL[k]
                value = roll_z(ya_send[step, m, j, pl.ds(PAD - ex, nx), :], ez)
                total = value if total is None else total + value
            oy[m] = total

    one = lambda i: pl.ds(i, 1)

    def pack_x(step):
        for m in range(2):
            xb_send[step, m, pl.ds(0, ny), :] = dens[leave_x[m]]
            for n in range(2):
                xb_send[step, m, one(ny + n), :] = oy[n, one(leave_x[m]), :]
        for c, (sx, sy) in enumerate(CORNERS):
            mx, my = (sx + 1) // 2, (sy + 1) // 2
            cb_send[step, c, 1:2, :] = dens[leave_x[mx], one(leave_y[my]), :]
            cb_send[step, c, 2:3, :] = oy[my, one(leave_x[mx]), :]
            cb_send[step, c, 3:4, :] = ox[mx, one(leave_y[my]), :]

    def pack_y(step):
        for m in range(2):
            for n in range(2):
                yb_send[step, m, 1, one(n), :] = ox[n, one(leave_y[m]), :]
            for x in range(nx):
                yb_send[step, m, 0, one(x), :] = dens[x, one(leave_y[m]), :]

    def pack_corners(step):
        for c, (sx, sy) in enumerate(CORNERS):
            mx, my = (sx + 1) // 2, (sy + 1) // 2
            j = CROSS[my].index(INDEX[(sx, sy, 0)])
            cb_send[step, c, 0:1, :] = ya_send[step, my, j, pl.ds(PAD + leave_x[mx], 1), :]

    def arrive(step, k, x, block, value):
        if step == STEPS - 1:
            fluid = mask_ref[x, block, :] == 1
            out_ref[k, x, block, :] = out_ref[k, x, block, :] + jnp.where(fluid, value, 0.0)
        else:
            f_buf[k, x, block, :] = f_buf[k, x, block, :] + value

    def x_arrive(step):
        for m in range(2):
            x = enter_x[m]
            for h in range(halves):
                block = pl.ds(8 * h, 8)
                total = None
                for j, k in enumerate(XK[m]):
                    _, ey, ez = VEL[k]
                    value = roll_z(xa_recv[step, m, j, pl.ds(PAD + 8 * h - ey, 8), :], ez)
                    arrive(step, k, x, block, value)
                    total = value if total is None else total + value
                if step < STEPS - 1:
                    dens[x, block, :] = dens[x, block, :] + total

    def y_arrive(step):
        for m in range(2):
            row = pl.ds(enter_y[m], 1)
            total = None
            for j, k in enumerate(CROSS[m]):
                ex, _, ez = VEL[k]
                value = roll_z(ya_recv[step, m, j, pl.ds(PAD - ex, nx), :], ez)
                y_tile[m, j] = value
                total = value if total is None else total + value
            y_tile[m, 5] = total
            for x in range(nx):
                for j, k in enumerate(CROSS[m]):
                    arrive(step, k, x, row, y_tile[m, j, pl.ds(x, 1), :])
                if step < STEPS - 1:
                    dens[x, row, :] = dens[x, row, :] + y_tile[m, 5, pl.ds(x, 1), :]

    def own_potential(x, h):
        block, where = pl.ds(8 * h, 8), pl.ds(PAD + 8 * h, 8)
        fluid = mask_ref[x, block, :] == 1
        value = 1.0 - jnp.exp(-dens[x, block, :])
        pot[0, x + 1, where, :] = jnp.where(fluid, value, pot[0, x + 1, where, :])

    def corners_arrive(step):
        for c, (sx, sy) in enumerate(CORNERS):
            mx, my = (sx + 1) // 2, (sy + 1) // 2
            x, y = enter_x[mx], enter_y[my]
            row = pl.ds(y, 1)
            value = cb_recv[step, c, 0:1, :]
            arrive(step, INDEX[(sx, sy, 0)], x, row, value)
            if step < STEPS - 1:
                dens[x, row, :] = dens[x, row, :] + value

    def ghost_potential(step):
        def put(x, where, density):
            flag = pot[1, x, where, :] == 1.0
            pot[0, x, where, :] = jnp.where(flag, 1.0 - jnp.exp(-density), pot[0, x, where, :])

        for m in range(2):
            gx_d[m] = xb_recv[step, m, pl.ds(0, ny), :] + ox[1 - m]
            gy_d[m] = yb_recv[step, m, 0] + oy[1 - m]
        for c, (sx, sy) in enumerate(CORNERS):
            mx, my = (sx + 1) // 2, (sy + 1) // 2
            x, y = enter_x[mx], enter_y[my]
            j = CROSS[my].index(INDEX[(-sx, sy, 0)])
            gx_d[mx, one(y), :] = gx_d[mx, one(y), :] + (
                ya_recv[step, my, j, one(PAD + x), :] + cb_recv[step, c, 2:3, :]
            )
            j = XK[mx].index(INDEX[(sx, -sy, 0)])
            gy_d[my, one(x), :] = gy_d[my, one(x), :] + (
                xa_recv[step, mx, j, one(PAD + y), :] + cb_recv[step, c, 3:4, :]
            )
            j = CROSS[1 - my].index(INDEX[(-sx, -sy, 0)])
            density = (
                cb_recv[step, c, 1:2, :] + ya_send[step, 1 - my, j, one(PAD + x), :]
            ) + (xb_recv[step, mx, one(ny + 1 - my), :] + yb_recv[step, my, 1, one(1 - mx), :])
            put(ghost_x[mx], one(ghost_y[my]), density)
        for m in range(2):
            for h in range(halves):
                put(ghost_x[m], pl.ds(PAD + 8 * h, 8), gx_d[m, pl.ds(8 * h, 8), :])
            gy_d[m] = 1.0 - jnp.exp(-gy_d[m])
            for x in range(nx):
                where = one(ghost_y[m])
                flag = pot[1, x + 1, where, :] == 1.0
                pot[0, x + 1, where, :] = jnp.where(
                    flag, gy_d[m, one(x), :], pot[0, x + 1, where, :]
                )

    for copy in fetches:
        copy.wait()
    for row in range(19):
        rate = rate_ref[row]
        coef[0, row] = 1.0 - rate
        coef[1, row] = rate * EQUIL_SCALE[row]
        coef[2, row] = (1.0 - 0.5 * rate) * SOURCE_SCALE[row]
    each_block(first)
    pl.semaphore_wait(barrier, len(SENDS))

    def start(group, swapped=()):
        if swapped:
            @pl.when(gx == counts[0] - 1)
            def _():
                for copy in swapped:
                    copy.start()

            @pl.when(gx != counts[0] - 1)
            def _():
                for copy in group:
                    copy.start()
        else:
            for copy in group:
                copy.start()
        return group

    def finish(group):
        for copy in group:
            copy.wait()

    def start_pot():
        group = pot_copies()
        order = [1, 0, 6, 7, 4, 5, 2, 3]
        return start([group[i] for i in order], [group[i] for i in (0, 1, 4, 5, 6, 7, 2, 3)])

    def start_a(step):
        group = a_copies(step, "x")
        return start(group, group[::-1])

    def start_b(step):
        group, corners = b_copies(step, "x"), b_copies(step, "corner")
        return start(group + corners[::-1], group[::-1] + corners)

    moving = start_pot()
    clear()
    finish(moving)
    pot_unpack()
    EDGE, NEXT, INNER = (0, 2, nx - 1), (1, 2, nx - 3), (2, nx - 4, 1)
    WITHIN = (1, nx - 2, 1)
    for step in range(STEPS):
        final = step == STEPS - 1
        hit = functools.partial(collision, step)
        move = functools.partial(stream, step)
        each_block(hit, *EDGE, group=2)
        x_moving = start_a(step)
        pack_corners(step)
        if not final:
            each_block(hit, *NEXT, group=2)
            if step == 0:
                each_block(inflow, *EDGE)
            each_block(move, *EDGE)
            x_sums(step)
            y_sums(step)
            pack_x(step)
        b_moving = start_b(step)
        if step == 0:
            each_block(inflow, *WITHIN)
        if final:
            each_block(hit, *NEXT, group=2)
        each_block(hit, *INNER, group=2)
        y_moving = start(a_copies(step, "y"))
        if final:
            leaving = [pltpu.make_async_copy(vel_ref, vel_hbm, out_sem.at[0])]
            leaving[0].start()
            each_block(move)
        else:
            each_block(move, *WITHIN)
            y_sums(step)
            pack_y(step)
            b_moving += start(b_copies(step, "y"))
        finish(y_moving)
        y_arrive(step)
        if final:
            for i, (x, count) in enumerate([(1, nx - 2), (0, 1), (nx - 1, 1)]):
                where = pl.ds(x, count)
                leaving.append(
                    pltpu.make_async_copy(
                        out_ref.at[:, where], out_hbm.at[:, where], out_sem.at[1 + i]
                    )
                )
            leaving[1].start()
        else:
            each_block(own_potential, *WITHIN)
        finish(x_moving)
        x_arrive(step)
        finish(b_moving)
        corners_arrive(step)
        if final:
            leaving[2].start()
            leaving[3].start()
            finish(leaving)
        else:
            each_block(own_potential, *EDGE)
            ghost_potential(step)


CHUNK = 5


def hand_over(pop_in, vel_in, pop_out, vel_out, pop, vel, in_sem, out_sem):
    parts = [(pop_in, pop, pop_out, k) for k in range(0, pop_in.shape[0], CHUNK)]
    parts.append((vel_in, vel, vel_out, 0))
    inward, outward = [], []
    for i, (src, held, dst, k) in enumerate(parts):
        where = pl.ds(k, min(CHUNK, src.shape[0] - k))
        inward.append(pltpu.make_async_copy(src.at[where], held.at[where], in_sem.at[i]))
        outward.append(pltpu.make_async_copy(held.at[where], dst.at[where], out_sem.at[i]))
    for copy in inward:
        copy.start()
    for arriving, leaving in zip(inward, outward):
        arriving.wait()
        leaving.start()
    for copy in outward:
        copy.wait()


def per_device(counts, populations, fluid_mask, wet_class, wall_potential, relax_rates):
    nx, ny, nz = fluid_mask.shape
    hbm = pl.BlockSpec(memory_space=pltpu.HBM)
    f32 = jnp.float32
    padded = (nx + 2, ny + 2 * PAD, nz)
    shapes = (
        jax.ShapeDtypeStruct((19, nx, ny, nz), f32),
        jax.ShapeDtypeStruct((3, nx, ny, nz), f32),
    )
    results = pl.pallas_call(
        functools.partial(kernel, counts),
        out_shape=shapes,
        in_specs=[hbm] * 5,
        out_specs=(hbm, hbm),
        scratch_shapes=[
            pltpu.VMEM((19, nx, ny, nz), f32),
            pltpu.VMEM((3, nx, ny, nz), f32),
            pltpu.VMEM(populations.shape, f32),
            pltpu.VMEM(fluid_mask.shape, jnp.int32),
            pltpu.VMEM(wet_class.shape, jnp.int32),
            pltpu.SMEM(wall_potential.shape, f32),
            pltpu.SMEM(relax_rates.shape, f32),
            pltpu.SMEM((3,) + relax_rates.shape, f32),
            pltpu.VMEM((2,) + padded, f32),
            pltpu.VMEM((19, nx, ny, nz), f32),
            pltpu.VMEM((nx, ny, nz), f32),
            pltpu.VMEM((nx, ny, nz), jnp.int32),
            pltpu.VMEM((2, 19) + padded, f32),
            pltpu.VMEM((2, 2, nx, nz), f32),
            pltpu.VMEM((2, 2, nx, nz), f32),
            pltpu.VMEM((4, 2, nx, nz), f32),
            pltpu.VMEM((STEPS, 2, 5, ny + 2 * PAD, nz), f32),
            pltpu.VMEM((STEPS, 2, 5, nx + 2 * PAD, nz), f32),
            pltpu.VMEM((STEPS, 2, 5, nx + 2 * PAD, nz), f32),
            pltpu.VMEM((STEPS, 2, ny + 8, nz), f32),
            pltpu.VMEM((STEPS, 2, ny + 8, nz), f32),
            pltpu.VMEM((STEPS, 2, 2, nx, nz), f32),
            pltpu.VMEM((STEPS, 2, 2, nx, nz), f32),
            pltpu.VMEM((STEPS, 4, 8, nz), f32),
            pltpu.VMEM((STEPS, 4, 8, nz), f32),
            pltpu.VMEM((2, ny, nz), f32),
            pltpu.VMEM((2, nx, nz), f32),
            pltpu.VMEM((2, ny, nz), f32),
            pltpu.VMEM((2, nx, nz), f32),
            pltpu.VMEM((2, 6, nx, nz), f32),
            pltpu.SemaphoreType.DMA((5,)),
            pltpu.SemaphoreType.DMA((4,)),
            pltpu.SemaphoreType.DMA((8,)),
            pltpu.SemaphoreType.DMA((8,)),
            pltpu.SemaphoreType.DMA((STEPS, 12)),
            pltpu.SemaphoreType.DMA((STEPS, 12)),
        ],
        compiler_params=pltpu.CompilerParams(
            collective_id=0, has_side_effects=True, vmem_limit_bytes=60 * 1024 * 1024
        ),
    )(populations, fluid_mask, wet_class, wall_potential, relax_rates)
    return pl.pallas_call(
        hand_over,
        out_shape=shapes,
        in_specs=[hbm] * 2,
        out_specs=(hbm, hbm),
        scratch_shapes=[pltpu.VMEM(shape.shape, f32) for shape in shapes]
        + [pltpu.SemaphoreType.DMA((-(-19 // CHUNK) + 1,))] * 2,
        compiler_params=pltpu.CompilerParams(vmem_limit_bytes=60 * 1024 * 1024),
    )(*results)


def solution(mesh):
    counts = (mesh.shape["gx"], mesh.shape["gy"])
    return jax.shard_map(
        functools.partial(per_device, counts),
        mesh=mesh,
        in_specs=(
            P(None, ("groups", "gx"), "gy", None),
            P(("groups", "gx"), "gy", None),
            P(("groups", "gx"), "gy", None),
            P("groups"),
            P(),
        ),
        out_specs=(P(None, ("groups", "gx"), "gy", None), P(None, ("groups", "gx"), "gy", None)),
        check_vma=False,
    )
```
